32 devices in a mesh: dp: 4 (over z), seq: 4 (over x, core), head: 2 (over y).
Axes of the slice: x: 2, y: 2, z: 4, core: 2. Of those that a mesh axis runs over, the one named last changes fastest.
Arguments:
- queries: bfloat16 [4, 1440, 512], P('dp', 'seq', 'head'), may hold values from -40 to 40
- key_rows: bfloat16 [4, 1440, 256], P('dp', 'seq', 'head'), may hold values from -6 to 6
- value_rows: bfloat16 [4, 1440, 256], P('dp', 'seq', 'head'), may hold values from -6 to 6
- grad_out: bfloat16 [4, 1440, 512], P('dp', 'seq', 'head'), may hold values from -6 to 6
- doc_lengths: int32 [4, 4], P('dp'), may hold values from 2 to 1080, as said below
- dest_index: int32 [4, 1440], P('dp', 'seq'), may hold values from 0 to 3, as said below
Outputs:
- attended: bfloat16 [4, 1440, 512], P('dp', 'seq', 'head')
- query_grad: bfloat16 [4, 1440, 512], P('dp', 'seq', 'head')
- key_grad: bfloat16 [4, 1440, 256], P('dp', 'seq', 'head')
- value_grad: bfloat16 [4, 1440, 256], P('dp', 'seq', 'head')
The draws below stay inside these ranges and needn't reach their ends.
Inputs may be any that keep to these rules, and one draw needn't show every extreme that they name: `dest_index`: within each loader sequence and each shard of 360 positions, every value 0 to 3 appears exactly 360 / 4 times. `doc_lengths`: each row holds 4 lengths that sum to 1440; the largest is exactly 1080.
All inputs are finite; a program needn't handle non-finite values.
Results may differ from the reference program's by a relative error of at most 0.0095.
Values may be sent and summed in bfloat16 or wider, within the bound.
No kernel may reach another device: no remote copies, remote signals or barrier semaphores. Data moves between devices by JAX's collectives and lax.ppermute only.
A program may use at most 64 MiB of HBM per device.

```python
import jax
import jax.numpy as jnp
from jax import lax

HEAD_DIM = 128
QHEADS = 4
KVHEADS = 2
WINDOW = 1024
ROWS = 360
SEQS = 4
LENGTH = 1440
MAXDOC = 1080


def doc_table(key):
    rest = LENGTH - MAXDOC

    def one_row(row_key):
        first_key, second_key, order_key = jax.random.split(row_key, 3)
        first = jax.random.randint(first_key, (), 2, rest // 2, dtype=jnp.int32)
        second = jax.random.randint(second_key, (), 2, rest // 4, dtype=jnp.int32)
        table = jnp.stack([jnp.asarray(MAXDOC, jnp.int32), first, second, rest - first - second])
        return table[jax.random.permutation(order_key, 4)]
    return jax.vmap(one_row)(jax.random.split(jax.random.fold_in(key, 11), SEQS))


def dest_table(key):
    span_count = LENGTH // ROWS
    group_rows = ROWS // SEQS
    row_keys = jax.random.split(jax.random.fold_in(key, 23), SEQS * span_count)
    ranking = jax.vmap(lambda row_key: jax.random.permutation(row_key, ROWS))(row_keys)
    return (ranking // group_rows).reshape(SEQS, LENGTH).astype(jnp.int32)


def draw_queries(key, part):
    shape = (SEQS, LENGTH, QHEADS * HEAD_DIM)
    noise = jax.random.normal(jax.random.fold_in(key, 3), shape, jnp.float32)
    return jnp.clip(2.0 * noise, -8.0, 8.0).astype(jnp.bfloat16)


def draw_key_rows(key, part):
    shape = (SEQS, LENGTH, KVHEADS * HEAD_DIM)
    noise = jax.random.normal(jax.random.fold_in(key, 5), shape, jnp.float32)
    return jnp.clip(noise, -6.0, 6.0).astype(jnp.bfloat16)


def draw_doc_lengths(key, part):
    return doc_table(key)


def draw_dest_index(key, part):
    return dest_table(key)


def steps_of(stream_key, dims, shards, low, high):
    gain, own = 1.0, jax.random.fold_in(stream_key, 6)
    for position, blocks in shards:
        draws = jnp.exp(jax.random.uniform(jax.random.fold_in(own, position), (blocks,), jnp.float32, low / len(shards), high / len(shards)))
        gain = gain * jnp.repeat(draws, dims[position] // blocks).reshape([-1 if axis == position else 1 for axis in range(len(dims))])
    return gain


def scatter_about(key, shape, spread, bound, cuts=(), kind=jnp.bfloat16):
    values = jax.random.normal(key, shape, jnp.float32) * spread
    if len(cuts) > 0:
        values = steps_of(key, shape, cuts, -0.22, 0.18) * values
    return jnp.clip(values, min=-bound, max=bound).astype(kind)


def setup_inputs(seed: int = 0) -> dict:
    key_of = jax.random.split(jax.random.key(seed), 7)
    queries = draw_queries(jax.random.fold_in(key_of[6], 71), 0)
    key_rows = draw_key_rows(jax.random.fold_in(key_of[6], 71), 0)
    value_rows = scatter_about(key_of[2], (SEQS, LENGTH, KVHEADS * HEAD_DIM), 1.0, 6.0, ((0, 4), (1, 4), (2, 2)))
    grad_out = scatter_about(key_of[3], (SEQS, LENGTH, QHEADS * HEAD_DIM), 1.0, 6.0, ((0, 4), (1, 4), (2, 2)))
    doc_lengths = draw_doc_lengths(jax.random.fold_in(key_of[6], 71), 0)
    dest_index = draw_dest_index(jax.random.fold_in(key_of[6], 71), 0)
    return {"queries": queries, "key_rows": key_rows, "value_rows": value_rows, "grad_out": grad_out, "doc_lengths": doc_lengths, "dest_index": dest_index}


score_scale = 168.0 ** -0.5
neg_large = -1e30


def document_ids(lengths):
    boundary = jnp.cumsum(lengths, dtype=jnp.int32)
    positions = jnp.arange(LENGTH, dtype=jnp.int32)
    return jnp.sum((positions[:, None] >= boundary[None, :]).astype(jnp.int32), axis=1)


def sorted_order(dest_index):
    seq_count = dest_index.shape[0]
    blocked = dest_index.reshape(seq_count, LENGTH // ROWS, ROWS)
    ranking = blocked * ROWS + jnp.arange(ROWS, dtype=jnp.int32)
    return jnp.argsort(ranking, axis=-1).astype(jnp.int32)


def balance(whole, send_order):
    seq_count = whole.shape[0]
    span_count = LENGTH // ROWS
    group_rows = ROWS // seq_count
    col_count = whole.shape[2]
    blocks = whole.reshape(seq_count, span_count, ROWS, col_count)
    ranked = jnp.take_along_axis(blocks, send_order[..., None], axis=2)
    ranked = ranked.reshape(seq_count, span_count, seq_count, group_rows, col_count)
    return jnp.transpose(ranked, (2, 1, 0, 3, 4)).reshape(seq_count, LENGTH, col_count)


def unbalance(whole, send_order):
    seq_count = whole.shape[0]
    span_count = LENGTH // ROWS
    group_rows = ROWS // seq_count
    col_count = whole.shape[2]
    ranked = whole.reshape(seq_count, span_count, seq_count, group_rows, col_count)
    ranked = jnp.transpose(ranked, (2, 1, 0, 3, 4)).reshape(seq_count, span_count, ROWS, col_count)
    back_order = jnp.argsort(send_order, axis=-1).astype(jnp.int32)
    restored = jnp.take_along_axis(ranked, back_order[..., None], axis=2)
    return restored.reshape(seq_count, LENGTH, col_count)


def group_pass(query_two, key_one, value_one, grad_two, doc_ids):
    positions = jnp.arange(LENGTH, dtype=jnp.int32)
    key_wide = key_one.astype(jnp.float32)
    value_wide = value_one.astype(jnp.float32)

    def shard_step(carry, shard_index):
        key_acc, value_acc = carry
        start_row = shard_index * ROWS
        query_block = lax.dynamic_slice_in_dim(query_two, start_row, ROWS, 0).astype(jnp.float32)
        grad_block = lax.dynamic_slice_in_dim(grad_two, start_row, ROWS, 0).astype(jnp.float32)
        query_pos = start_row + jnp.arange(ROWS, dtype=jnp.int32)
        query_docs = lax.dynamic_slice_in_dim(doc_ids, start_row, ROWS, 0)
        distance = query_pos[:, None] - positions[None, :]
        allowed = (query_docs[:, None] == doc_ids[None, :]) & (distance >= 0) & (distance < WINDOW)
        scores = jnp.einsum("qhd,kd->hqk", query_block, key_wide) * score_scale
        scores = jnp.where(allowed[None], scores, neg_large)
        row_peak = jnp.max(scores, axis=2, keepdims=True)
        weights = jnp.where(allowed[None], jnp.exp(scores - row_peak), 0.0)
        prob_rows = weights / jnp.sum(weights, axis=2, keepdims=True)
        prob_low = lax.optimization_barrier(prob_rows.astype(jnp.bfloat16)).astype(jnp.float32)
        mixed_rows = jnp.einsum("hqk,kd->qhd", prob_low, value_wide).astype(jnp.bfloat16)
        value_part = jnp.einsum("hqk,qhd->kd", prob_low, grad_block)
        prob_grad = jnp.einsum("qhd,kd->hqk", grad_block, value_wide)
        center = jnp.sum(prob_rows * prob_grad, axis=2, keepdims=True)
        dscore = (prob_rows * (prob_grad - center) * score_scale).astype(jnp.bfloat16)
        dscore = lax.optimization_barrier(dscore).astype(jnp.float32)
        query_grad = jnp.einsum("hqk,kd->qhd", dscore, key_wide).astype(jnp.bfloat16)
        key_part = jnp.einsum("hqk,qhd->kd", dscore, query_block)
        key_low = lax.optimization_barrier(key_part.astype(jnp.bfloat16)).astype(jnp.float32)
        value_low = lax.optimization_barrier(value_part.astype(jnp.bfloat16)).astype(jnp.float32)
        return (key_acc + key_low, value_acc + value_low), (mixed_rows, query_grad)

    zero_rows = jnp.zeros((LENGTH, HEAD_DIM), jnp.float32)
    totals, blocks = lax.scan(shard_step, (zero_rows, zero_rows), jnp.arange(LENGTH // ROWS, dtype=jnp.int32))
    attended = blocks[0].reshape(LENGTH, 2, HEAD_DIM)
    query_grad = blocks[1].reshape(LENGTH, 2, HEAD_DIM)
    return attended, query_grad, totals[0].astype(jnp.bfloat16), totals[1].astype(jnp.bfloat16)


def one_sequence(inputs):
    query_seq, key_seq, value_seq, grad_seq, lengths = inputs
    doc_ids = document_ids(lengths)
    head_pairs = key_seq.shape[1] // HEAD_DIM
    query_split = jnp.transpose(query_seq.reshape(LENGTH, head_pairs, 2, HEAD_DIM), (1, 0, 2, 3))
    grad_split = jnp.transpose(grad_seq.reshape(LENGTH, head_pairs, 2, HEAD_DIM), (1, 0, 2, 3))
    key_split = jnp.transpose(key_seq.reshape(LENGTH, head_pairs, HEAD_DIM), (1, 0, 2))
    value_split = jnp.transpose(value_seq.reshape(LENGTH, head_pairs, HEAD_DIM), (1, 0, 2))

    def per_group(member):
        return group_pass(member[0], member[1], member[2], member[3], doc_ids)

    result = lax.map(per_group, (query_split, key_split, value_split, grad_split))
    attended = jnp.transpose(result[0], (1, 0, 2, 3)).reshape(LENGTH, head_pairs * 2 * HEAD_DIM)
    query_grad = jnp.transpose(result[1], (1, 0, 2, 3)).reshape(LENGTH, head_pairs * 2 * HEAD_DIM)
    key_grad = jnp.transpose(result[2], (1, 0, 2)).reshape(LENGTH, head_pairs * HEAD_DIM)
    value_grad = jnp.transpose(result[3], (1, 0, 2)).reshape(LENGTH, head_pairs * HEAD_DIM)
    return attended, query_grad, key_grad, value_grad


def reference(queries, key_rows, value_rows, grad_out, doc_lengths, dest_index):
    send_order = sorted_order(dest_index)
    query_bal = balance(queries, send_order)
    key_bal = balance(key_rows, send_order)
    value_bal = balance(value_rows, send_order)
    grad_bal = balance(grad_out, send_order)
    outcome = lax.map(one_sequence, (query_bal, key_bal, value_bal, grad_bal, doc_lengths))
    return (unbalance(outcome[0], send_order), unbalance(outcome[1], send_order), unbalance(outcome[2], send_order), unbalance(outcome[3], send_order))
```

```python
import functools
import math

import jax
import jax.numpy as jnp
from jax import lax
from jax.experimental import pallas as pl
from jax.experimental.pallas import tpu as pltpu
from jax.sharding import PartitionSpec as P

HEAD_DIM = 128
WINDOW = 1024
TILE = 16
LANES = 128

score_scale = 168.0 ** (-0.5)
log2_e = 1.4426950408889634
neg_large = -1e30
vmem_bytes = 24 * 1024 * 1024
brief = pl.CostEstimate(flops=1, bytes_accessed=1, transcendentals=0)
pause = pl.CostEstimate(flops=10**11, bytes_accessed=10**8, transcendentals=0)

F32 = jnp.float32
BF16 = jnp.bfloat16
NT = (((1,), (1,)), ((), ()))
TN = (((0,), (0,)), ((), ()))


def dot(a, b, dims=(((1,), (0,)), ((), ()))):
    return lax.dot_general(a, b, dims, preferred_element_type=F32)


def receiver_of(me, step, peers):
    return me ^ step if peers & (peers - 1) == 0 else (me + step) % peers


def travel_order(peers):
    return list(range(2, peers)) + [1, 0]


def step_to(me, other, peers):
    if peers & (peers - 1) == 0:
        return other ^ me
    step = other - me
    return jnp.where(step < 0, step + peers, step)


def position_of(row, pad, group_rows):
    group, inner = row // pad, row % pad
    last = group_rows - 1
    return group * group_rows + (min(inner, last) if isinstance(row, int) else jnp.minimum(inner, last)), inner


def query_positions(rows, pad, row_count):
    lane = lax.broadcasted_iota(jnp.int32, (1, 2 * rows), 1)
    row = lane // (2 * LANES) * LANES + lane % LANES
    return position_of(row, pad, row_count * pad // rows)[0]


def stacked_row(row, head, unit):
    return pl.multiple_of(row // LANES * (2 * LANES) + head * LANES + row % LANES, unit)


def load(pairs, sems):
    copies = [pltpu.make_async_copy(*pair, sems.at[i]) for i, pair in enumerate(pairs)]
    for copy in copies:
        copy.start()
    return copies


def place_of(slot, slots):
    here = lax.broadcasted_iota(jnp.int32, (slots, slot.shape[1]), 0) == slot
    return here.astype(F32).astype(BF16)


def sort_kernel(peers, pad, dest_hbm, k_hbm, v_hbm, *refs):
    outs, slot_ref = refs[:peers], refs[peers]
    dest_ref, k_ref, v_ref, sems = refs[peers + 1 :]
    copies = load(((dest_hbm, dest_ref), (k_hbm, k_ref), (v_hbm, v_ref)), sems)
    rows = k_ref.shape[0]
    me = lax.axis_index("dp")
    wide = -(-peers // TILE) * TILE
    lane = lax.broadcasted_iota(jnp.int32, (wide, rows), 0)
    upto = (
        lax.broadcasted_iota(jnp.int32, (rows, rows), 0)
        <= lax.broadcasted_iota(jnp.int32, (rows, rows), 1)
    ).astype(F32)
    copies[0].wait()
    member = (lane == step_to(me, dest_ref[...], peers)).astype(F32)
    count = dot(member.astype(BF16), upto.astype(BF16))
    slot = jnp.sum(member * (count + (lane * pad - 1).astype(F32)), axis=0, keepdims=True)
    slot = slot.astype(jnp.int32)
    slot_ref[...] = slot
    place = place_of(slot, peers * pad)
    for copy, ref, at in zip(copies[1:], (k_ref, v_ref), (0, 1)):
        copy.wait()
        moved = dot(place, ref[...]).astype(BF16)
        for p in range(peers):
            outs[p][:, at * HEAD_DIM : (at + 1) * HEAD_DIM] = moved[p * pad : (p + 1) * pad]


def follow_kernel(peers, pad, slot_ref, lengths_hbm, q_hbm, g_hbm, *refs):
    outs, first_ref = refs[:peers], refs[peers]
    lengths_ref, q_ref, g_ref, sems = refs[peers + 1 :]
    copies = load(((q_hbm, q_ref), (g_hbm, g_ref), (lengths_hbm, lengths_ref)), sems)
    rows = q_ref.shape[0]
    place = place_of(slot_ref[...], peers * pad)
    for copy, ref, at in zip(copies, (q_ref, g_ref), (0, 2)):
        copy.wait()
        moved = dot(place, ref[...]).astype(BF16)
        for p in range(peers):
            outs[p][:, at * HEAD_DIM : (at + 2) * HEAD_DIM] = moved[p * pad : (p + 1) * pad]
    copies[2].wait()
    query_pos = query_positions(peers * pad, pad, rows) + lax.axis_index("seq") * rows
    first = jnp.maximum(query_pos - (WINDOW - 1), 0)
    edge = jnp.int32(0)
    for e in range(lengths_ref.shape[1]):
        edge = edge + lengths_ref[0, e]
        first = jnp.maximum(first, jnp.where(edge <= query_pos, edge, 0))
    first_ref[...] = first


def back_kernel(slot_ref, back_ref):
    rows, slots = back_ref.shape
    slot = slot_ref[...]
    eye = lax.broadcasted_iota(jnp.int32, (rows, rows), 0) == lax.broadcasted_iota(
        jnp.int32, (rows, rows), 1
    )
    column = jnp.sum(jnp.where(eye, slot, 0), axis=1, keepdims=True)
    back_ref[...] = (
        (lax.broadcasted_iota(jnp.int32, (rows, slots), 1) == column).astype(F32).astype(BF16)
    )


def windows(here, rows, pad, row_count):
    group_rows = row_count // (rows // pad)
    blocks = []
    for b in range(rows // LANES):
        reach = here * row_count + position_of(b * LANES, pad, group_rows)[0] - (WINDOW - 1)
        reach = max(reach, 0)
        row = reach // row_count * rows + reach % row_count // group_rows * pad + reach % group_rows
        keys = slice(row // LANES * LANES, here * rows + (b + 1) * LANES)
        blocks.append((keys, slice(2 * b * LANES, 2 * (b + 1) * LANES)))
    return blocks


def attend_kernel(peers, pad, row_count, span, sequence_ref, q_ref, g_ref, first_ref, *refs):
    own_grad_ref, far_grad_ref, low_ref, ds_ref = refs[:4]
    w_scr, dp_scr, dv_scr, dk_scr = refs[4:]
    rows = peers * pad
    shard = lax.axis_index("seq")
    factor = score_scale * log2_e
    first, last = first_ref[...], query_positions(rows, pad, row_count)
    group_rows = row_count // peers
    offset, inner = position_of(lax.broadcasted_iota(jnp.int32, (rows, 1), 0), pad, group_rows)
    offset = jnp.where(inner < group_rows, offset, -(2**24))

    def attend(here):
        blocks = windows(here, rows, pad, row_count)

        def strips(window):
            at = window.start
            while at < window.stop:
                end = min(at - at % rows + rows, window.stop)
                yield at // rows, slice(at, end), slice(at % rows, at % rows + end - at)
                at = end

        def products(window, cols):
            w_scr[window, cols] = dot(sequence_ref[window, :HEAD_DIM], q_ref[cols, :], NT)
            dp_scr[window, cols] = dot(sequence_ref[window, HEAD_DIM:], g_ref[cols, :], NT)

        def weigh(window, cols):
            parts = []
            for c, at, inside in strips(window):
                allowed = offset[inside] >= first[:, cols] - c * row_count
                if c == here:
                    allowed = allowed & (offset[inside] <= last[:, cols])
                part = jnp.where(allowed, w_scr[at, cols], neg_large)
                w_scr[at, cols] = part
                parts.append(jnp.max(part, axis=0, keepdims=True))
            peak = functools.reduce(jnp.maximum, parts)
            total, mean = 0.0, 0.0
            for _, at, _ in strips(window):
                w = jnp.exp2((w_scr[at, cols] - peak) * factor)
                w_scr[at, cols] = w
                total += jnp.sum(w, axis=0, keepdims=True)
                mean += jnp.sum(w * dp_scr[at, cols], axis=0, keepdims=True)
            share = 1.0 / total
            center = mean * share
            for _, at, _ in strips(window):
                p = w_scr[at, cols] * share
                low_ref[at, cols] = p.astype(BF16)
                ds_ref[at, cols] = (p * (dp_scr[at, cols] - center)).astype(BF16)

        def spread(window, cols, start):
            dv = dot(low_ref[window, cols], g_ref[cols, :])
            dk = dot(ds_ref[window, cols], q_ref[cols, :])
            old = slice(window.start, start)
            if start > window.start:
                dv_scr[old, :] += dv[: start - window.start]
                dk_scr[old, :] += dk[: start - window.start]
            dv_scr[start : window.stop, :] = dv[start - window.start :]
            dk_scr[start : window.stop, :] = dk[start - window.start :]

        products(*blocks[0])
        start = blocks[0][0].start
        for b, (window, cols) in enumerate(blocks):
            if b + 1 < len(blocks):
                products(*blocks[b + 1])
            weigh(window, cols)
            spread(window, cols, start)
            start = window.stop
        for c in range(span):
            grad, half = ((own_grad_ref, 0), (far_grad_ref, 0), (own_grad_ref, 1), (far_grad_ref, 1))[here ^ c]
            to, at = slice(half * rows, (half + 1) * rows), slice(c * rows, (c + 1) * rows)
            if c <= here and at.stop > blocks[0][0].start:
                grad[to, HEAD_DIM:] = dv_scr[at, :].astype(BF16)
                grad[to, :HEAD_DIM] = (dk_scr[at, :] * score_scale).astype(BF16)
            else:
                grad[to, :] = jnp.zeros((rows, 2 * HEAD_DIM), BF16)

    for here in range(span):
        pl.when(shard == here)(functools.partial(attend, here))


def gather_kernel(peers, pad, row_count, span, sequence_ref, low_ref, ds_ref, *refs):
    out_refs, turned_scr, whole_scr = refs[:peers], refs[peers], refs[peers + 1]
    rows = peers * pad
    me = lax.axis_index("dp")
    shard = lax.axis_index("seq")

    def gather(here):
        for window, cols in windows(here, rows, pad, row_count):
            turned_scr[:HEAD_DIM, cols] = dot(sequence_ref[window, HEAD_DIM:], low_ref[window, cols], TN)
            turned_scr[HEAD_DIM:, cols] = (
                dot(sequence_ref[window, :HEAD_DIM], ds_ref[window, cols], TN) * score_scale
            )

    for here in range(span):
        pl.when(shard == here)(functools.partial(gather, here))

    unit = math.gcd(pad, LANES)
    for column in range(2):
        whole_scr[...] = turned_scr[column * HEAD_DIM : (column + 1) * HEAD_DIM, :].T.astype(BF16)
        for p in range(peers):
            for t in range(pad // unit):
                for h in range(2):
                    at = pl.ds(stacked_row(step_to(p, me, peers) * pad + t * unit, h, unit), unit)
                    to = (2 * column + h) * HEAD_DIM
                    out_refs[p][t * unit : (t + 1) * unit, to : to + HEAD_DIM] = whole_scr[at, :]


def settle_kernel(peers, back_ref, *refs):
    pieces, outs = refs[:peers], refs[peers:]
    order = travel_order(peers)
    whole = jnp.concatenate([pieces[order.index(p)][...] for p in range(peers)], axis=0)
    settled = dot(back_ref[...], whole).astype(BF16)
    at = 0
    for out in outs:
        out[...] = settled[:, at : at + out.shape[1]]
        at += out.shape[1]


def join_kernel(peers, *refs):
    whole = refs[-1]
    pad = refs[0].shape[0]
    me = lax.axis_index("dp")
    for step, ref in zip(travel_order(peers), refs):
        whole[pl.ds(pl.multiple_of(step_to(step, me, peers) * pad, pad), pad), :] = ref[...]


def stack_kernel(peers, *refs):
    stacks = refs[peers:]
    pad = refs[0].shape[0]
    unit = math.gcd(pad, LANES)
    me = lax.axis_index("dp")
    for step, ref in zip(travel_order(peers), refs):
        for t in range(pad // unit):
            for h in range(2):
                to = pl.ds(stacked_row(step_to(step, me, peers) * pad + t * unit, h, unit), unit)
                for column, out in enumerate(stacks):
                    at = (2 * column + h) * HEAD_DIM
                    out[to, :] = ref[t * unit : (t + 1) * unit, at : at + HEAD_DIM]


def part_kernel(peers, a_ref, b_ref, *outs):
    pad = outs[0].shape[0]
    me = lax.axis_index("dp")
    for step, out in enumerate(outs):
        at = pl.ds(pl.multiple_of(step_to(step, me, peers) * pad, pad), pad)
        out[...] = (a_ref[at, :] + b_ref[at, :].astype(F32)).astype(BF16)


def add_kernel(a_ref, b_ref, after_ref, *outs):
    at = 0
    for out in outs:
        size = out.shape[0]
        both = a_ref[at : at + size, :].astype(F32) + b_ref[at : at + size, :].astype(F32)
        out[...] = both.astype(out.dtype)
        at += size


def call(kernel, outs, *args, scratch=(), in_specs=None, cost=None):
    return pl.pallas_call(
        kernel,
        out_shape=outs,
        in_specs=in_specs or [pl.BlockSpec(memory_space=pltpu.VMEM)] * len(args),
        scratch_shapes=scratch,
        compiler_params=pltpu.CompilerParams(vmem_limit_bytes=vmem_bytes),
        cost_estimate=cost,
    )(*args)


def local(queries, key_rows, value_rows, grad_out, doc_lengths, dest_index):
    row_count = queries.shape[1]
    peers = lax.axis_size("dp")
    span = lax.axis_size("seq")
    group_rows = row_count // peers
    pad = -(-group_rows // TILE) * TILE
    rows = peers * pad
    shape = jax.ShapeDtypeStruct

    sources = [
        pltpu.with_memory_space_constraint(a, pltpu.HBM)
        for a in (doc_lengths, dest_index, queries[0], key_rows[0], value_rows[0], grad_out[0])
    ]
    in_hbm = pl.BlockSpec(memory_space=pltpu.HBM)
    in_vmem = pl.BlockSpec(memory_space=pltpu.VMEM)

    def loaded(*arrays):
        return [pltpu.VMEM(a.shape, a.dtype) for a in arrays]

    lengths, dest, q, k, v, g = sources
    *kv, slot = call(
        functools.partial(sort_kernel, peers, pad),
        [shape((pad, 2 * HEAD_DIM), BF16)] * peers + [shape((1, row_count), jnp.int32)],
        dest,
        k,
        v,
        in_specs=[in_hbm] * 3,
        scratch=loaded(dest, k, v) + [pltpu.SemaphoreType.DMA((3,))],
    )
    *qg, first_seen = call(
        functools.partial(follow_kernel, peers, pad),
        [shape((pad, 4 * HEAD_DIM), BF16)] * peers + [shape((1, 2 * rows), jnp.int32)],
        slot,
        lengths,
        q,
        g,
        in_specs=[in_vmem] + [in_hbm] * 3,
        scratch=[pltpu.SMEM(lengths.shape, jnp.int32)]
        + loaded(q, g)
        + [pltpu.SemaphoreType.DMA((3,))],
        cost=pause,
    )

    def exchange(pieces, home=False):
        arrived = []
        for k in travel_order(peers):
            way = [(i, receiver_of(i, k, peers)) for i in range(peers)]
            if home:
                way = [(j, i) for i, j in way]
            arrived.append(lax.ppermute(pieces[k], "dp", way) if k else pieces[k])
        return arrived

    def to_partner(values, distance):
        return lax.ppermute(values, "seq", [(i, i ^ distance) for i in range(span)])

    def join(pieces):
        return call(functools.partial(join_kernel, peers), shape((rows, 2 * HEAD_DIM), BF16), *pieces, cost=brief)

    kv = exchange(kv)
    qg = exchange(qg)
    sequence = lax.all_gather(join(kv), "seq", axis=0, tiled=True)
    tall = shape((2 * rows, HEAD_DIM), BF16)
    stacked = call(
        functools.partial(stack_kernel, peers),
        [tall, tall],
        *qg,
        cost=brief,
    )

    back = call(back_kernel, shape((row_count, rows), BF16), slot)

    wide = (span * rows, 2 * rows)
    own_grad, far_grad, low, ds = call(
        functools.partial(attend_kernel, peers, pad, row_count, span),
        [shape((2 * rows, 2 * HEAD_DIM), BF16)] * 2 + [shape(wide, BF16)] * 2,
        sequence,
        *stacked,
        first_seen,
        scratch=[pltpu.VMEM(wide, F32)] * 2 + [pltpu.VMEM((span * rows, HEAD_DIM), F32)] * 2,
    )
    attended = call(
        functools.partial(gather_kernel, peers, pad, row_count, span),
        [shape((pad, 4 * HEAD_DIM), BF16)] * peers,
        sequence,
        low,
        ds,
        scratch=[pltpu.VMEM((2 * HEAD_DIM, 2 * rows), F32), pltpu.VMEM((2 * rows, HEAD_DIM), BF16)],
    )

    attended = exchange(attended, home=True)
    returned = to_partner(far_grad, 1)
    half = shape((rows, 2 * HEAD_DIM), BF16)
    mine, theirs = call(add_kernel, [shape(half.shape, F32), half], own_grad, returned, attended[-1], cost=pause)
    theirs = to_partner(theirs, 2)
    pair_grad = call(
        functools.partial(part_kernel, peers),
        [shape((pad, 2 * HEAD_DIM), BF16)] * peers,
        mine,
        theirs,
        cost=pause,
    )
    pair_grad = exchange(pair_grad, home=True)

    wide, narrow = shape((row_count, 2 * HEAD_DIM), BF16), shape((row_count, HEAD_DIM), BF16)
    first = call(
        functools.partial(settle_kernel, peers), [wide, wide], back, *attended
    )
    last = call(functools.partial(settle_kernel, peers), [narrow, narrow], back, *pair_grad)
    return first[0][None], first[1][None], last[0][None], last[1][None]


def solution(mesh):
    split = P("dp", "seq", "head")
    return jax.shard_map(
        local,
        mesh=mesh,
        in_specs=(split, split, split, split, P("dp", None), P("dp", "seq")),
        out_specs=(split, split, split, split),
        check_vma=False,
    )
```

```python
import functools
import math

import jax
import jax.numpy as jnp
from jax import lax
from jax.experimental import pallas as pl
from jax.experimental.pallas import tpu as pltpu
from jax.sharding import PartitionSpec as P

HEAD_DIM = 128
WINDOW = 1024
TILE = 16
LANES = 128
PARTS = 2

score_scale = 168.0 ** (-0.5)
log2_e = 1.4426950408889634
neg_large = -1e30
vmem_bytes = 24 * 1024 * 1024
brief = pl.CostEstimate(flops=1, bytes_accessed=1, transcendentals=0)
pause = pl.CostEstimate(flops=10**11, bytes_accessed=10**8, transcendentals=0)

F32 = jnp.float32
BF16 = jnp.bfloat16
NT = (((1,), (1,)), ((), ()))
TN = (((0,), (0,)), ((), ()))


def dot(a, b, dims=(((1,), (0,)), ((), ()))):
    return lax.dot_general(a, b, dims, preferred_element_type=F32)


def receiver_of(me, step, peers):
    return me ^ step if peers & (peers - 1) == 0 else (me + step) % peers


def travel_order(peers):
    return list(range(2, peers)) + [1, 0]


def step_to(me, other, peers):
    if peers & (peers - 1) == 0:
        return other ^ me
    step = other - me
    return jnp.where(step < 0, step + peers, step)


def position_of(row, pad, group_rows):
    group, inner = row // pad, row % pad
    last = group_rows - 1
    return group * group_rows + (min(inner, last) if isinstance(row, int) else jnp.minimum(inner, last)), inner


def query_positions(rows, pad, row_count):
    lane = lax.broadcasted_iota(jnp.int32, (1, 2 * rows), 1)
    row = lane // (2 * LANES) * LANES + lane % LANES
    return position_of(row, pad, row_count * pad // rows)[0]


def stacked_row(row, head, unit):
    return pl.multiple_of(row // LANES * (2 * LANES) + head * LANES + row % LANES, unit)


def place_of(slot, slots):
    here = lax.broadcasted_iota(jnp.int32, (slots, slot.shape[1]), 0) == slot
    return here.astype(F32).astype(BF16)


def sort_kernel(peers, pad, lengths_hbm, dest_hbm, k_hbm, v_hbm, q_hbm, g_hbm, *refs):
    outs, slot_ref, first_ref, q_ref, g_ref = refs[:peers], *refs[peers : peers + 4]
    lengths_ref, dest_ref, k_ref, v_ref, sems = refs[peers + 4 :]
    loads = (
        (dest_hbm, dest_ref),
        (k_hbm, k_ref),
        (v_hbm, v_ref),
        (lengths_hbm, lengths_ref),
        (q_hbm, q_ref),
        (g_hbm, g_ref),
    )
    copies = [pltpu.make_async_copy(*pair, sems.at[i]) for i, pair in enumerate(loads)]
    for copy in copies:
        copy.start()
    rows = k_ref.shape[0]
    me = lax.axis_index("dp")
    wide = -(-peers // TILE) * TILE
    lane = lax.broadcasted_iota(jnp.int32, (wide, rows), 0)
    upto = (
        lax.broadcasted_iota(jnp.int32, (rows, rows), 0)
        <= lax.broadcasted_iota(jnp.int32, (rows, rows), 1)
    ).astype(F32)
    copies[0].wait()
    member = (lane == step_to(me, dest_ref[...], peers)).astype(F32)
    count = dot(member.astype(BF16), upto.astype(BF16))
    slot = jnp.sum(member * (count + (lane * pad - 1).astype(F32)), axis=0, keepdims=True)
    slot = slot.astype(jnp.int32)
    slot_ref[...] = slot
    place = place_of(slot, peers * pad)
    for copy, ref, at in zip(copies[1:3], (k_ref, v_ref), (0, 1)):
        copy.wait()
        moved = dot(place, ref[...]).astype(BF16)
        for p in range(peers):
            outs[p][:, at * HEAD_DIM : (at + 1) * HEAD_DIM] = moved[p * pad : (p + 1) * pad]
    copies[3].wait()
    query_pos = query_positions(peers * pad, pad, rows) + lax.axis_index("seq") * rows
    first = jnp.maximum(query_pos - (WINDOW - 1), 0)
    edge = jnp.int32(0)
    for e in range(lengths_ref.shape[1]):
        edge = edge + lengths_ref[0, e]
        first = jnp.maximum(first, jnp.where(edge <= query_pos, edge, 0))
    first_ref[...] = first
    for copy in copies[4:]:
        copy.wait()


def follow_kernel(peers, pad, slot_ref, q_ref, g_ref, *outs):
    place = place_of(slot_ref[...], peers * pad)
    for ref, at in ((q_ref, 0), (g_ref, 2)):
        moved = dot(place, ref[...]).astype(BF16)
        for p in range(peers):
            outs[p][:, at * HEAD_DIM : (at + 2) * HEAD_DIM] = moved[p * pad : (p + 1) * pad]


def back_kernel(slot_ref, back_ref):
    rows, slots = back_ref.shape
    slot = slot_ref[...]
    eye = lax.broadcasted_iota(jnp.int32, (rows, rows), 0) == lax.broadcasted_iota(
        jnp.int32, (rows, rows), 1
    )
    column = jnp.sum(jnp.where(eye, slot, 0), axis=1, keepdims=True)
    back_ref[...] = (
        (lax.broadcasted_iota(jnp.int32, (rows, slots), 1) == column).astype(F32).astype(BF16)
    )


def windows(here, rows, pad, row_count):
    group_rows = row_count // (rows // pad)
    blocks = []
    for b in range(rows // LANES):
        reach = here * row_count + position_of(b * LANES, pad, group_rows)[0] - (WINDOW - 1)
        reach = max(reach, 0)
        row = reach // row_count * rows + reach % row_count // group_rows * pad + reach % group_rows
        keys = slice(row // LANES * LANES, here * rows + (b + 1) * LANES)
        blocks.append((keys, slice(2 * b * LANES, 2 * (b + 1) * LANES)))
    return blocks


def attend_kernel(peers, pad, row_count, span, sequence_ref, q_ref, g_ref, first_ref, *refs):
    own_grad_ref, far_grad_ref, low_ref, ds_ref = refs[:4]
    w_scr, dp_scr, dv_scr, dk_scr = refs[4:]
    rows = peers * pad
    shard = lax.axis_index("seq")
    factor = score_scale * log2_e
    first, last = first_ref[...], query_positions(rows, pad, row_count)
    group_rows = row_count // peers
    offset, inner = position_of(lax.broadcasted_iota(jnp.int32, (rows, 1), 0), pad, group_rows)
    offset = jnp.where(inner < group_rows, offset, -(2**24))

    def attend(here):
        blocks = windows(here, rows, pad, row_count)

        def strips(window):
            at = window.start
            while at < window.stop:
                end = min(at - at % rows + rows, window.stop)
                yield at // rows, slice(at, end), slice(at % rows, at % rows + end - at)
                at = end

        def products(window, cols):
            w_scr[window, cols] = dot(sequence_ref[window, :HEAD_DIM], q_ref[cols, :], NT)
            dp_scr[window, cols] = dot(sequence_ref[window, HEAD_DIM:], g_ref[cols, :], NT)

        def weigh(window, cols):
            parts = []
            for c, at, inside in strips(window):
                allowed = offset[inside] >= first[:, cols] - c * row_count
                if c == here:
                    allowed = allowed & (offset[inside] <= last[:, cols])
                part = jnp.where(allowed, w_scr[at, cols], neg_large)
                w_scr[at, cols] = part
                parts.append(jnp.max(part, axis=0, keepdims=True))
            peak = functools.reduce(jnp.maximum, parts)
            total, mean = 0.0, 0.0
            for _, at, _ in strips(window):
                w = jnp.exp2((w_scr[at, cols] - peak) * factor)
                w_scr[at, cols] = w
                total += jnp.sum(w, axis=0, keepdims=True)
                mean += jnp.sum(w * dp_scr[at, cols], axis=0, keepdims=True)
            share = 1.0 / total
            center = mean * share
            for _, at, _ in strips(window):
                p = w_scr[at, cols] * share
                low_ref[at, cols] = p.astype(BF16)
                ds_ref[at, cols] = (p * (dp_scr[at, cols] - center)).astype(BF16)

        def spread(window, cols, start):
            dv = dot(low_ref[window, cols], g_ref[cols, :])
            dk = dot(ds_ref[window, cols], q_ref[cols, :])
            old = slice(window.start, start)
            if start > window.start:
                dv_scr[old, :] += dv[: start - window.start]
                dk_scr[old, :] += dk[: start - window.start]
            dv_scr[start : window.stop, :] = dv[start - window.start :]
            dk_scr[start : window.stop, :] = dk[start - window.start :]

        products(*blocks[0])
        start = blocks[0][0].start
        for b, (window, cols) in enumerate(blocks):
            if b + 1 < len(blocks):
                products(*blocks[b + 1])
            weigh(window, cols)
            spread(window, cols, start)
            start = window.stop
        for c in range(span):
            grad, half = ((own_grad_ref, 0), (far_grad_ref, 0), (own_grad_ref, 1), (far_grad_ref, 1))[here ^ c]
            to, at = slice(half * rows, (half + 1) * rows), slice(c * rows, (c + 1) * rows)
            if c <= here and at.stop > blocks[0][0].start:
                grad[to, HEAD_DIM:] = dv_scr[at, :].astype(BF16)
                grad[to, :HEAD_DIM] = (dk_scr[at, :] * score_scale).astype(BF16)
            else:
                grad[to, :] = jnp.zeros((rows, 2 * HEAD_DIM), BF16)

    for here in range(span):
        pl.when(shard == here)(functools.partial(attend, here))


def gather_kernel(peers, pad, row_count, span, sequence_ref, low_ref, ds_ref, *refs):
    out_refs, turned_scr, whole_scr = refs[:peers], refs[peers], refs[peers + 1]
    rows = peers * pad
    me = lax.axis_index("dp")
    shard = lax.axis_index("seq")

    def gather(here):
        for window, cols in windows(here, rows, pad, row_count):
            turned_scr[:HEAD_DIM, cols] = dot(sequence_ref[window, HEAD_DIM:], low_ref[window, cols], TN)
            turned_scr[HEAD_DIM:, cols] = (
                dot(sequence_ref[window, :HEAD_DIM], ds_ref[window, cols], TN) * score_scale
            )

    for here in range(span):
        pl.when(shard == here)(functools.partial(gather, here))

    unit = math.gcd(pad, LANES)
    for column in range(2):
        whole_scr[...] = turned_scr[column * HEAD_DIM : (column + 1) * HEAD_DIM, :].T.astype(BF16)
        for p in range(peers):
            for t in range(pad // unit):
                for h in range(2):
                    at = pl.ds(stacked_row(step_to(p, me, peers) * pad + t * unit, h, unit), unit)
                    to = (2 * column + h) * HEAD_DIM
                    out_refs[p][t * unit : (t + 1) * unit, to : to + HEAD_DIM] = whole_scr[at, :]


def settle_kernel(peers, back_ref, *refs):
    pieces, outs = refs[:peers], refs[peers:]
    order = travel_order(peers)
    whole = jnp.concatenate([pieces[order.index(p)][...] for p in range(peers)], axis=0)
    settled = dot(back_ref[...], whole).astype(BF16)
    at = 0
    for out in outs:
        out[...] = settled[:, at : at + out.shape[1]]
        at += out.shape[1]


def join_kernel(peers, *refs):
    whole = refs[-1]
    pad = refs[0].shape[0]
    me = lax.axis_index("dp")
    for step, ref in zip(travel_order(peers), refs):
        whole[pl.ds(pl.multiple_of(step_to(step, me, peers) * pad, pad), pad), :] = ref[...]


def stack_kernel(order, *refs):
    peers = len(order)
    stacks = refs[peers:]
    pad = refs[0].shape[0]
    unit = math.gcd(pad, LANES)
    me = lax.axis_index("dp")
    for step, ref in zip(order, refs):
        for t in range(pad // unit):
            for h in range(2):
                to = pl.ds(stacked_row(step_to(step, me, peers) * pad + t * unit, h, unit), unit)
                for column, out in enumerate(stacks):
                    at = (2 * column + h) * HEAD_DIM
                    out[to, :] = ref[t * unit : (t + 1) * unit, at : at + HEAD_DIM]


def pair_kernel(peers, own_ref, returned_ref, after_ref, *outs):
    rows = own_ref.shape[0] // 2
    pad = rows // peers
    me = lax.axis_index("dp")
    for half in range(2):
        for step in range(peers):
            row = half * rows + step_to(step, me, peers) * pad
            at = pl.ds(pl.multiple_of(row, pad), pad)
            both = own_ref[at, :].astype(F32) + returned_ref[at, :].astype(F32)
            if half == 0:
                outs[0][step * pad : (step + 1) * pad, :] = both
            else:
                part, place = divmod(step * pad, outs[1].shape[0])
                outs[1 + part][place : place + pad, :] = both.astype(BF16)


def sum_kernel(parts, mine_ref, *refs):
    theirs, outs = refs[:parts], refs[parts + 1 :]
    pad = outs[0].shape[0]
    for step, out in enumerate(outs):
        part, place = divmod(step * pad, theirs[0].shape[0])
        out[...] = (
            mine_ref[step * pad : (step + 1) * pad, :]
            + theirs[part][place : place + pad, :].astype(F32)
        ).astype(BF16)


def call(kernel, outs, *args, scratch=(), in_specs=None, cost=None):
    return pl.pallas_call(
        kernel,
        out_shape=outs,
        in_specs=in_specs or [pl.BlockSpec(memory_space=pltpu.VMEM)] * len(args),
        scratch_shapes=scratch,
        compiler_params=pltpu.CompilerParams(vmem_limit_bytes=vmem_bytes),
        cost_estimate=cost,
    )(*args)


def local(queries, key_rows, value_rows, grad_out, doc_lengths, dest_index):
    row_count = queries.shape[1]
    peers = lax.axis_size("dp")
    span = lax.axis_size("seq")
    group_rows = row_count // peers
    pad = -(-group_rows // TILE) * TILE
    rows = peers * pad
    shape = jax.ShapeDtypeStruct

    sources = [
        pltpu.with_memory_space_constraint(a, pltpu.HBM)
        for a in (doc_lengths, dest_index, queries[0], key_rows[0], value_rows[0], grad_out[0])
    ]
    lengths, dest, q, k, v, g = sources
    *kv, slot, first_seen, q, g = call(
        functools.partial(sort_kernel, peers, pad),
        [shape((pad, 2 * HEAD_DIM), BF16)] * peers
        + [shape((1, row_count), jnp.int32), shape((1, 2 * rows), jnp.int32)]
        + [shape(q.shape, BF16)] * 2,
        lengths,
        dest,
        k,
        v,
        q,
        g,
        in_specs=[pl.BlockSpec(memory_space=pltpu.HBM)] * 6,
        scratch=[pltpu.SMEM(lengths.shape, jnp.int32), pltpu.VMEM(dest.shape, jnp.int32)]
        + [pltpu.VMEM(k.shape, BF16)] * 2
        + [pltpu.SemaphoreType.DMA((6,))],
    )
    qg = call(
        functools.partial(follow_kernel, peers, pad),
        [shape((pad, 4 * HEAD_DIM), BF16)] * peers,
        slot,
        q,
        g,
        cost=pause,
    )

    def exchange(pieces, home=False, order=travel_order(peers)):
        arrived = []
        for k in order:
            way = [(i, receiver_of(i, k, peers)) for i in range(peers)]
            if home:
                way = [(j, i) for i, j in way]
            arrived.append(lax.ppermute(pieces[k], "dp", way) if k else pieces[k])
        return arrived

    def to_partner(values, distance):
        return lax.ppermute(values, "seq", [(i, i ^ distance) for i in range(span)])

    def join(pieces):
        return call(functools.partial(join_kernel, peers), shape((rows, 2 * HEAD_DIM), BF16), *pieces, cost=brief)

    kv = exchange(kv)
    near_first = [1, *range(peers - 1, 1, -1), 0]
    qg = exchange(qg, order=near_first)
    sequence = lax.all_gather(join(kv), "seq", axis=0, tiled=True)
    tall = shape((2 * rows, HEAD_DIM), BF16)
    stacked = call(
        functools.partial(stack_kernel, near_first),
        [tall, tall],
        *qg,
        cost=brief,
    )

    back = call(back_kernel, shape((row_count, rows), BF16), slot)

    wide = (span * rows, 2 * rows)
    own_grad, far_grad, low, ds = call(
        functools.partial(attend_kernel, peers, pad, row_count, span),
        [shape((2 * rows, 2 * HEAD_DIM), BF16)] * 2 + [shape(wide, BF16)] * 2,
        sequence,
        *stacked,
        first_seen,
        scratch=[pltpu.VMEM(wide, F32)] * 2 + [pltpu.VMEM((span * rows, HEAD_DIM), F32)] * 2,
    )
    attended = call(
        functools.partial(gather_kernel, peers, pad, row_count, span),
        [shape((pad, 4 * HEAD_DIM), BF16)] * peers,
        sequence,
        low,
        ds,
        scratch=[pltpu.VMEM((2 * HEAD_DIM, 2 * rows), F32), pltpu.VMEM((2 * rows, HEAD_DIM), BF16)],
    )

    returned = to_partner(far_grad, 1)
    parts = PARTS
    mine, *theirs = call(
        functools.partial(pair_kernel, peers),
        [shape((rows, 2 * HEAD_DIM), F32)] + [shape((rows // parts, 2 * HEAD_DIM), BF16)] * parts,
        own_grad,
        returned,
        attended[0],
        cost=pause,
    )
    attended = exchange(attended, home=True)
    pair_grad = call(
        functools.partial(sum_kernel, parts),
        [shape((pad, 2 * HEAD_DIM), BF16)] * peers,
        mine,
        *[to_partner(part, 2) for part in theirs],
        attended[0],
        cost=pause,
    )
    pair_grad = exchange(pair_grad, home=True)

    wide, narrow = shape((row_count, 2 * HEAD_DIM), BF16), shape((row_count, HEAD_DIM), BF16)
    first = call(
        functools.partial(settle_kernel, peers), [wide, wide], back, *attended
    )
    last = call(functools.partial(settle_kernel, peers), [narrow, narrow], back, *pair_grad)
    return first[0][None], first[1][None], last[0][None], last[1][None]


def solution(mesh):
    split = P("dp", "seq", "head")
    return jax.shard_map(
        local,
        mesh=mesh,
        in_specs=(split, split, split, split, P("dp", None), P("dp", "seq")),
        out_specs=(split, split, split, split),
        check_vma=False,
    )
```

```python
import functools
import math

import jax
import jax.numpy as jnp
from jax import lax
from jax.experimental import pallas as pl
from jax.experimental.pallas import tpu as pltpu
from jax.sharding import PartitionSpec as P

HEAD_DIM = 128
WINDOW = 1024
TILE = 16
LANES = 128
PARTS = 2

score_scale = 168.0 ** (-0.5)
log2_e = 1.4426950408889634
neg_large = -1e30
vmem_bytes = 24 * 1024 * 1024
brief = pl.CostEstimate(flops=1, bytes_accessed=1, transcendentals=0)
pause = pl.CostEstimate(flops=10**11, bytes_accessed=10**8, transcendentals=0)

F32 = jnp.float32
BF16 = jnp.bfloat16
NT = (((1,), (1,)), ((), ()))
TN = (((0,), (0,)), ((), ()))


def dot(a, b, dims=(((1,), (0,)), ((), ()))):
    return lax.dot_general(a, b, dims, preferred_element_type=F32)


def receiver_of(me, step, peers):
    return me ^ step if peers & (peers - 1) == 0 else (me + step) % peers


def travel_order(peers):
    return list(range(2, peers)) + [1, 0]


def step_to(me, other, peers):
    if peers & (peers - 1) == 0:
        return other ^ me
    step = other - me
    return jnp.where(step < 0, step + peers, step)


def position_of(row, pad, group_rows):
    group, inner = row // pad, row % pad
    last = group_rows - 1
    return group * group_rows + (min(inner, last) if isinstance(row, int) else jnp.minimum(inner, last)), inner


def query_positions(rows, pad, row_count):
    lane = lax.broadcasted_iota(jnp.int32, (1, 2 * rows), 1)
    row = lane // (2 * LANES) * LANES + lane % LANES
    return position_of(row, pad, row_count * pad // rows)[0]


def stacked_row(row, head, unit):
    return pl.multiple_of(row // LANES * (2 * LANES) + head * LANES + row % LANES, unit)


def place_of(slot, slots):
    here = lax.broadcasted_iota(jnp.int32, (slots, slot.shape[1]), 0) == slot
    return here.astype(F32).astype(BF16)


def sort_kernel(peers, pad, lengths_hbm, dest_hbm, k_hbm, v_hbm, q_hbm, g_hbm, *refs):
    outs, slot_ref, first_ref, q_ref, g_ref = refs[:peers], *refs[peers : peers + 4]
    lengths_ref, dest_ref, k_ref, v_ref, sems = refs[peers + 4 :]
    loads = (
        (dest_hbm, dest_ref),
        (k_hbm, k_ref),
        (v_hbm, v_ref),
        (lengths_hbm, lengths_ref),
        (q_hbm, q_ref),
        (g_hbm, g_ref),
    )
    copies = [pltpu.make_async_copy(*pair, sems.at[i]) for i, pair in enumerate(loads)]
    for copy in copies:
        copy.start()
    rows = k_ref.shape[0]
    me = lax.axis_index("dp")
    wide = -(-peers // TILE) * TILE
    lane = lax.broadcasted_iota(jnp.int32, (wide, rows), 0)
    upto = (
        lax.broadcasted_iota(jnp.int32, (rows, rows), 0)
        <= lax.broadcasted_iota(jnp.int32, (rows, rows), 1)
    ).astype(F32)
    copies[0].wait()
    member = (lane == step_to(me, dest_ref[...], peers)).astype(F32)
    count = dot(member.astype(BF16), upto.astype(BF16))
    slot = jnp.sum(member * (count + (lane * pad - 1).astype(F32)), axis=0, keepdims=True)
    slot = slot.astype(jnp.int32)
    slot_ref[...] = slot
    place = place_of(slot, peers * pad)
    for copy, ref, at in zip(copies[1:3], (k_ref, v_ref), (0, 1)):
        copy.wait()
        moved = dot(place, ref[...]).astype(BF16)
        for p in range(peers):
            outs[p][:, at * HEAD_DIM : (at + 1) * HEAD_DIM] = moved[p * pad : (p + 1) * pad]
    copies[3].wait()
    query_pos = query_positions(peers * pad, pad, rows) + lax.axis_index("seq") * rows
    first = jnp.maximum(query_pos - (WINDOW - 1), 0)
    edge = jnp.int32(0)
    for e in range(lengths_ref.shape[1]):
        edge = edge + lengths_ref[0, e]
        first = jnp.maximum(first, jnp.where(edge <= query_pos, edge, 0))
    first_ref[...] = first
    for copy in copies[4:]:
        copy.wait()


def follow_kernel(peers, pad, slot_ref, q_ref, g_ref, *outs):
    place = place_of(slot_ref[...], peers * pad)
    for ref, at in ((q_ref, 0), (g_ref, 2)):
        moved = dot(place, ref[...]).astype(BF16)
        for p in range(peers):
            outs[p][:, at * HEAD_DIM : (at + 2) * HEAD_DIM] = moved[p * pad : (p + 1) * pad]


def back_kernel(slot_ref, back_ref):
    rows, slots = back_ref.shape
    slot = slot_ref[...]
    eye = lax.broadcasted_iota(jnp.int32, (rows, rows), 0) == lax.broadcasted_iota(
        jnp.int32, (rows, rows), 1
    )
    column = jnp.sum(jnp.where(eye, slot, 0), axis=1, keepdims=True)
    back_ref[...] = (
        (lax.broadcasted_iota(jnp.int32, (rows, slots), 1) == column).astype(F32).astype(BF16)
    )


def windows(here, rows, pad, row_count):
    group_rows = row_count // (rows // pad)
    blocks = []
    for b in range(rows // LANES):
        reach = here * row_count + position_of(b * LANES, pad, group_rows)[0] - (WINDOW - 1)
        reach = max(reach, 0)
        row = reach // row_count * rows + reach % row_count // group_rows * pad + reach % group_rows
        keys = slice(row // LANES * LANES, here * rows + (b + 1) * LANES)
        blocks.append((keys, slice(2 * b * LANES, 2 * (b + 1) * LANES)))
    return blocks


def attend_kernel(peers, pad, row_count, span, sequence_ref, q_ref, g_ref, first_ref, *refs):
    own_grad_ref, far_grad_ref, low_ref, ds_ref = refs[:4]
    w_scr, dp_scr, dv_scr, dk_scr = refs[4:]
    rows = peers * pad
    shard = lax.axis_index("seq")
    factor = score_scale * log2_e
    first, last = first_ref[...], query_positions(rows, pad, row_count)
    group_rows = row_count // peers
    offset, inner = position_of(lax.broadcasted_iota(jnp.int32, (rows, 1), 0), pad, group_rows)
    offset = jnp.where(inner < group_rows, offset, -(2**24))

    def attend(here):
        blocks = windows(here, rows, pad, row_count)

        def strips(window):
            at = window.start
            while at < window.stop:
                end = min(at - at % rows + rows, window.stop)
                yield at // rows, slice(at, end), slice(at % rows, at % rows + end - at)
                at = end

        def tiles(window):
            for c, at, inside in strips(window):
                for i in range(0, at.stop - at.start, 64):
                    yield c, slice(at.start + i, at.start + i + 64), slice(inside.start + i, inside.start + i + 64)

        def fold(x):
            return x.reshape(-1, 8, x.shape[1])

        def products(window, cols):
            dp_scr[window, cols] = dot(sequence_ref[window, HEAD_DIM:], g_ref[cols, :], NT)
            scores = dot(sequence_ref[window, :HEAD_DIM], q_ref[cols, :], NT)
            peak8 = jnp.full((8, cols.stop - cols.start), neg_large, F32)
            for c, at, inside in tiles(window):
                allowed = offset[inside] >= first[:, cols] - c * row_count
                if c == here and inside.stop > cols.start // 2:
                    allowed = allowed & (offset[inside] <= last[:, cols])
                part = scores[at.start - window.start : at.stop - window.start]
                part = jnp.where(allowed, part, neg_large)
                w_scr[at, cols] = part
                peak8 = jnp.maximum(peak8, jnp.max(fold(part), axis=0))
            return jnp.max(peak8, axis=0, keepdims=True)

        def weigh(window, cols, peak):
            width = cols.stop - cols.start
            total8 = jnp.zeros((8, width), F32)
            mean8 = jnp.zeros((8, width), F32)
            for _, at, _ in tiles(window):
                w = jnp.exp2((w_scr[at, cols] - peak) * factor)
                w_scr[at, cols] = w
                total8 += jnp.sum(fold(w), axis=0)
                mean8 += jnp.sum(fold(w * dp_scr[at, cols]), axis=0)
            share = 1.0 / jnp.sum(total8, axis=0, keepdims=True)
            center = jnp.sum(mean8, axis=0, keepdims=True) * share
            for _, at, _ in tiles(window):
                p = w_scr[at, cols] * share
                low_ref[at, cols] = p.astype(BF16)
                ds_ref[at, cols] = (p * (dp_scr[at, cols] - center)).astype(BF16)

        def spread(window, cols, start):
            dv = dot(low_ref[window, cols], g_ref[cols, :])
            dk = dot(ds_ref[window, cols], q_ref[cols, :])
            old = slice(window.start, start)
            if start > window.start:
                dv_scr[old, :] += dv[: start - window.start]
                dk_scr[old, :] += dk[: start - window.start]
            dv_scr[start : window.stop, :] = dv[start - window.start :]
            dk_scr[start : window.stop, :] = dk[start - window.start :]

        start = blocks[0][0].start
        peak = products(*blocks[0])
        starts = [blocks[0][0].start] + [window.stop for window, _ in blocks]
        for b, (window, cols) in enumerate(blocks):
            after = products(*blocks[b + 1]) if b + 1 < len(blocks) else None
            if b:
                spread(*blocks[b - 1], starts[b - 1])
            weigh(window, cols, peak)
            peak = after
        spread(*blocks[-1], starts[len(blocks) - 1])
        for c in range(span):
            grad, half = ((own_grad_ref, 0), (far_grad_ref, 0), (own_grad_ref, 1), (far_grad_ref, 1))[here ^ c]
            to, at = slice(half * rows, (half + 1) * rows), slice(c * rows, (c + 1) * rows)
            if c <= here and at.stop > blocks[0][0].start:
                grad[to, HEAD_DIM:] = dv_scr[at, :].astype(BF16)
                grad[to, :HEAD_DIM] = (dk_scr[at, :] * score_scale).astype(BF16)
            else:
                grad[to, :] = jnp.zeros((rows, 2 * HEAD_DIM), BF16)

    for here in range(span):
        pl.when(shard == here)(functools.partial(attend, here))


def gather_kernel(peers, pad, row_count, span, sequence_ref, low_ref, ds_ref, *refs):
    out_refs, turned_scr, whole_scr = refs[:peers], refs[peers], refs[peers + 1]
    rows = peers * pad
    me = lax.axis_index("dp")
    shard = lax.axis_index("seq")

    def gather(here):
        for window, cols in windows(here, rows, pad, row_count):
            turned_scr[:HEAD_DIM, cols] = dot(sequence_ref[window, HEAD_DIM:], low_ref[window, cols], TN)
            turned_scr[HEAD_DIM:, cols] = (
                dot(sequence_ref[window, :HEAD_DIM], ds_ref[window, cols], TN) * score_scale
            )

    for here in range(span):
        pl.when(shard == here)(functools.partial(gather, here))

    unit = math.gcd(pad, LANES)
    for column in range(2):
        whole_scr[...] = turned_scr[column * HEAD_DIM : (column + 1) * HEAD_DIM, :].T.astype(BF16)
        for p in range(peers):
            for t in range(pad // unit):
                for h in range(2):
                    at = pl.ds(stacked_row(step_to(p, me, peers) * pad + t * unit, h, unit), unit)
                    to = (2 * column + h) * HEAD_DIM
                    out_refs[p][t * unit : (t + 1) * unit, to : to + HEAD_DIM] = whole_scr[at, :]


def settle_kernel(peers, back_ref, *refs):
    pieces, outs = refs[:peers], refs[peers:]
    order = travel_order(peers)
    whole = jnp.concatenate([pieces[order.index(p)][...] for p in range(peers)], axis=0)
    settled = dot(back_ref[...], whole).astype(BF16)
    at = 0
    for out in outs:
        out[...] = settled[:, at : at + out.shape[1]]
        at += out.shape[1]


def join_kernel(peers, *refs):
    whole = refs[-1]
    pad = refs[0].shape[0]
    me = lax.axis_index("dp")
    for step, ref in zip(travel_order(peers), refs):
        whole[pl.ds(pl.multiple_of(step_to(step, me, peers) * pad, pad), pad), :] = ref[...]


def stack_kernel(order, *refs):
    peers = len(order)
    stacks = refs[peers:]
    pad = refs[0].shape[0]
    unit = math.gcd(pad, LANES)
    me = lax.axis_index("dp")
    for step, ref in zip(order, refs):
        for t in range(pad // unit):
            for h in range(2):
                to = pl.ds(stacked_row(step_to(step, me, peers) * pad + t * unit, h, unit), unit)
                for column, out in enumerate(stacks):
                    at = (2 * column + h) * HEAD_DIM
                    out[to, :] = ref[t * unit : (t + 1) * unit, at : at + HEAD_DIM]


def pair_kernel(peers, own_ref, returned_ref, after_ref, *outs):
    rows = own_ref.shape[0] // 2
    pad = rows // peers
    me = lax.axis_index("dp")
    for half in range(2):
        for step in range(peers):
            row = half * rows + step_to(step, me, peers) * pad
            at = pl.ds(pl.multiple_of(row, pad), pad)
            both = own_ref[at, :].astype(F32) + returned_ref[at, :].astype(F32)
            if half == 0:
                outs[0][step * pad : (step + 1) * pad, :] = both
            else:
                part, place = divmod(step * pad, outs[1].shape[0])
                outs[1 + part][place : place + pad, :] = both.astype(BF16)


def sum_kernel(parts, mine_ref, *refs):
    theirs, outs = refs[:parts], refs[parts + 1 :]
    pad = outs[0].shape[0]
    for step, out in enumerate(outs):
        part, place = divmod(step * pad, theirs[0].shape[0])
        out[...] = (
            mine_ref[step * pad : (step + 1) * pad, :]
            + theirs[part][place : place + pad, :].astype(F32)
        ).astype(BF16)


def call(kernel, outs, *args, scratch=(), in_specs=None, cost=None):
    return pl.pallas_call(
        kernel,
        out_shape=outs,
        in_specs=in_specs or [pl.BlockSpec(memory_space=pltpu.VMEM)] * len(args),
        scratch_shapes=scratch,
        compiler_params=pltpu.CompilerParams(vmem_limit_bytes=vmem_bytes),
        cost_estimate=cost,
    )(*args)


def local(queries, key_rows, value_rows, grad_out, doc_lengths, dest_index):
    row_count = queries.shape[1]
    peers = lax.axis_size("dp")
    span = lax.axis_size("seq")
    group_rows = row_count // peers
    pad = -(-group_rows // TILE) * TILE
    rows = peers * pad
    shape = jax.ShapeDtypeStruct

    sources = [
        pltpu.with_memory_space_constraint(a, pltpu.HBM)
        for a in (doc_lengths, dest_index, queries[0], key_rows[0], value_rows[0], grad_out[0])
    ]
    lengths, dest, q, k, v, g = sources
    *kv, slot, first_seen, q, g = call(
        functools.partial(sort_kernel, peers, pad),
        [shape((pad, 2 * HEAD_DIM), BF16)] * peers
        + [shape((1, row_count), jnp.int32), shape((1, 2 * rows), jnp.int32)]
        + [shape(q.shape, BF16)] * 2,
        lengths,
        dest,
        k,
        v,
        q,
        g,
        in_specs=[pl.BlockSpec(memory_space=pltpu.HBM)] * 6,
        scratch=[pltpu.SMEM(lengths.shape, jnp.int32), pltpu.VMEM(dest.shape, jnp.int32)]
        + [pltpu.VMEM(k.shape, BF16)] * 2
        + [pltpu.SemaphoreType.DMA((6,))],
    )
    qg = call(
        functools.partial(follow_kernel, peers, pad),
        [shape((pad, 4 * HEAD_DIM), BF16)] * peers,
        slot,
        q,
        g,
        cost=pause,
    )

    def exchange(pieces, home=False, order=travel_order(peers)):
        arrived = []
        for k in order:
            way = [(i, receiver_of(i, k, peers)) for i in range(peers)]
            if home:
                way = [(j, i) for i, j in way]
            arrived.append(lax.ppermute(pieces[k], "dp", way) if k else pieces[k])
        return arrived

    def to_partner(values, distance):
        return lax.ppermute(values, "seq", [(i, i ^ distance) for i in range(span)])

    def join(pieces):
        return call(functools.partial(join_kernel, peers), shape((rows, 2 * HEAD_DIM), BF16), *pieces, cost=brief)

    kv = exchange(kv)
    near_first = [1, *range(peers - 1, 1, -1), 0]
    qg = exchange(qg, order=near_first)
    sequence = lax.all_gather(join(kv), "seq", axis=0, tiled=True)
    tall = shape((2 * rows, HEAD_DIM), BF16)
    stacked = call(
        functools.partial(stack_kernel, near_first),
        [tall, tall],
        *qg,
        cost=brief,
    )

    back = call(back_kernel, shape((row_count, rows), BF16), slot)

    wide = (span * rows, 2 * rows)
    own_grad, far_grad, low, ds = call(
        functools.partial(attend_kernel, peers, pad, row_count, span),
        [shape((2 * rows, 2 * HEAD_DIM), BF16)] * 2 + [shape(wide, BF16)] * 2,
        sequence,
        *stacked,
        first_seen,
        scratch=[pltpu.VMEM(wide, F32)] * 2 + [pltpu.VMEM((span * rows, HEAD_DIM), F32)] * 2,
    )
    attended = call(
        functools.partial(gather_kernel, peers, pad, row_count, span),
        [shape((pad, 4 * HEAD_DIM), BF16)] * peers,
        sequence,
        low,
        ds,
        scratch=[pltpu.VMEM((2 * HEAD_DIM, 2 * rows), F32), pltpu.VMEM((2 * rows, HEAD_DIM), BF16)],
    )

    returned = to_partner(far_grad, 1)
    parts = PARTS
    mine, *theirs = call(
        functools.partial(pair_kernel, peers),
        [shape((rows, 2 * HEAD_DIM), F32)] + [shape((rows // parts, 2 * HEAD_DIM), BF16)] * parts,
        own_grad,
        returned,
        attended[0],
        cost=pause,
    )
    attended = exchange(attended, home=True)
    pair_grad = call(
        functools.partial(sum_kernel, parts),
        [shape((pad, 2 * HEAD_DIM), BF16)] * peers,
        mine,
        *[to_partner(part, 2) for part in theirs],
        attended[0],
        cost=pause,
    )
    pair_grad = exchange(pair_grad, home=True)

    wide, narrow = shape((row_count, 2 * HEAD_DIM), BF16), shape((row_count, HEAD_DIM), BF16)
    first = call(
        functools.partial(settle_kernel, peers), [wide, wide], back, *attended
    )
    last = call(functools.partial(settle_kernel, peers), [narrow, narrow], back, *pair_grad)
    return first[0][None], first[1][None], last[0][None], last[1][None]


def solution(mesh):
    split = P("dp", "seq", "head")
    return jax.shard_map(
        local,
        mesh=mesh,
        in_specs=(split, split, split, split, P("dp", None), P("dp", "seq")),
        out_specs=(split, split, split, split),
        check_vma=False,
    )
```

```python
import functools
import math

import jax
import jax.numpy as jnp
from jax import lax
from jax.experimental import pallas as pl
from jax.experimental.pallas import tpu as pltpu
from jax.sharding import PartitionSpec as P

HEAD_DIM = 128
WINDOW = 1024
TILE = 16
LANES = 128
PARTS = 2

score_scale = 168.0 ** (-0.5)
log2_e = 1.4426950408889634
neg_large = -1e30
vmem_bytes = 24 * 1024 * 1024
brief = pl.CostEstimate(flops=1, bytes_accessed=1, transcendentals=0)
pause = pl.CostEstimate(flops=10**11, bytes_accessed=10**8, transcendentals=0)

F32 = jnp.float32
BF16 = jnp.bfloat16
NT = (((1,), (1,)), ((), ()))
TN = (((0,), (0,)), ((), ()))


def dot(a, b, dims=(((1,), (0,)), ((), ()))):
    return lax.dot_general(a, b, dims, preferred_element_type=F32)


def receiver_of(me, step, peers):
    return me ^ step if peers & (peers - 1) == 0 else (me + step) % peers


def travel_order(peers):
    return list(range(2, peers)) + [1, 0]


def step_to(me, other, peers):
    if peers & (peers - 1) == 0:
        return other ^ me
    step = other - me
    return jnp.where(step < 0, step + peers, step)


def position_of(row, pad, group_rows):
    group, inner = row // pad, row % pad
    last = group_rows - 1
    return group * group_rows + (min(inner, last) if isinstance(row, int) else jnp.minimum(inner, last)), inner


def query_positions(rows, pad, row_count):
    lane = lax.broadcasted_iota(jnp.int32, (1, 2 * rows), 1)
    row = lane // (2 * LANES) * LANES + lane % LANES
    return position_of(row, pad, row_count * pad // rows)[0]


def stacked_row(row, head, unit):
    return pl.multiple_of(row // LANES * (2 * LANES) + head * LANES + row % LANES, unit)


def place_of(slot, slots):
    here = lax.broadcasted_iota(jnp.int32, (slots, slot.shape[1]), 0) == slot
    return here.astype(F32).astype(BF16)


def sort_kernel(peers, pad, lengths_hbm, dest_hbm, k_hbm, v_hbm, q_hbm, g_hbm, *refs):
    outs, slot_ref, first_ref, q_ref, g_ref = refs[:peers], *refs[peers : peers + 4]
    lengths_ref, dest_ref, kv_ref, sems = refs[peers + 4 :]
    loads = (
        (dest_hbm, dest_ref),
        (k_hbm, kv_ref.at[:, :HEAD_DIM]),
        (v_hbm, kv_ref.at[:, HEAD_DIM:]),
        (lengths_hbm, lengths_ref),
        (q_hbm, q_ref),
        (g_hbm, g_ref),
    )
    copies = [pltpu.make_async_copy(*pair, sems.at[i]) for i, pair in enumerate(loads)]
    for copy in copies:
        copy.start()
    rows = kv_ref.shape[0]
    me = lax.axis_index("dp")
    wide = -(-peers // TILE) * TILE
    lane = lax.broadcasted_iota(jnp.int32, (wide, rows), 0)
    upto = (
        lax.broadcasted_iota(jnp.int32, (rows, rows), 0)
        <= lax.broadcasted_iota(jnp.int32, (rows, rows), 1)
    ).astype(F32)
    copies[0].wait()
    member = (lane == step_to(me, dest_ref[...], peers)).astype(F32)
    count = dot(member.astype(BF16), upto.astype(BF16))
    slot = jnp.sum(member * (count + (lane * pad - 1).astype(F32)), axis=0, keepdims=True)
    slot = slot.astype(jnp.int32)
    slot_ref[...] = slot
    place = place_of(slot, peers * pad)
    for copy in copies[1:3]:
        copy.wait()
    moved = dot(place, kv_ref[...]).astype(BF16)
    for p in range(peers):
        outs[p][...] = moved[p * pad : (p + 1) * pad]
    copies[3].wait()
    query_pos = query_positions(peers * pad, pad, rows) + lax.axis_index("seq") * rows
    first = jnp.maximum(query_pos - (WINDOW - 1), 0)
    edge = jnp.int32(0)
    for e in range(lengths_ref.shape[1]):
        edge = edge + lengths_ref[0, e]
        first = jnp.maximum(first, jnp.where(edge <= query_pos, edge, 0))
    first_ref[...] = first
    for copy in copies[4:]:
        copy.wait()


def follow_kernel(peers, pad, slot_ref, q_ref, g_ref, *outs):
    place = place_of(slot_ref[...], peers * pad)
    for ref, at in ((q_ref, 0), (g_ref, 2)):
        moved = dot(place, ref[...]).astype(BF16)
        for p in range(peers):
            outs[p][:, at * HEAD_DIM : (at + 2) * HEAD_DIM] = moved[p * pad : (p + 1) * pad]


def back_kernel(slot_ref, back_ref):
    rows, slots = back_ref.shape
    slot = slot_ref[...]
    eye = lax.broadcasted_iota(jnp.int32, (rows, rows), 0) == lax.broadcasted_iota(
        jnp.int32, (rows, rows), 1
    )
    column = jnp.sum(jnp.where(eye, slot, 0), axis=1, keepdims=True)
    back_ref[...] = (
        (lax.broadcasted_iota(jnp.int32, (rows, slots), 1) == column).astype(F32).astype(BF16)
    )


def windows(here, rows, pad, row_count):
    group_rows = row_count // (rows // pad)
    blocks = []
    for b in range(rows // LANES):
        reach = here * row_count + position_of(b * LANES, pad, group_rows)[0] - (WINDOW - 1)
        reach = max(reach, 0)
        row = reach // row_count * rows + reach % row_count // group_rows * pad + reach % group_rows
        keys = slice(row // LANES * LANES, here * rows + (b + 1) * LANES)
        blocks.append((keys, slice(2 * b * LANES, 2 * (b + 1) * LANES)))
    return blocks


def stack(order, pieces, stacks):
    peers = len(order)
    pad = pieces[0].shape[0]
    unit = math.gcd(pad, LANES)
    me = lax.axis_index("dp")
    for step, piece in zip(order, pieces):
        for t in range(pad // unit):
            for h in range(2):
                to = pl.ds(stacked_row(step_to(step, me, peers) * pad + t * unit, h, unit), unit)
                for column, out in enumerate(stacks):
                    at = (2 * column + h) * HEAD_DIM
                    out[to, :] = piece[t * unit : (t + 1) * unit, at : at + HEAD_DIM]


def attend_kernel(order, pad, row_count, span, sequence_ref, first_ref, *refs):
    peers = len(order)
    own_grad_ref, far_grad_ref, low_ref, ds_ref = refs[peers : peers + 4]
    w_scr, dp_scr, dv_scr, dk_scr, q_ref, g_ref = refs[peers + 4 :]
    stack(order, refs[:peers], (q_ref, g_ref))
    rows = peers * pad
    shard = lax.axis_index("seq")
    factor = score_scale * log2_e
    first, last = first_ref[...], query_positions(rows, pad, row_count)
    group_rows = row_count // peers
    offset, inner = position_of(lax.broadcasted_iota(jnp.int32, (rows, 1), 0), pad, group_rows)
    offset = jnp.where(inner < group_rows, offset, -(2**24))

    def attend(here):
        blocks = windows(here, rows, pad, row_count)

        def strips(window):
            at = window.start
            while at < window.stop:
                end = min(at - at % rows + rows, window.stop)
                yield at // rows, slice(at, end), slice(at % rows, at % rows + end - at)
                at = end

        def tiles(window):
            for c, at, inside in strips(window):
                for i in range(0, at.stop - at.start, 64):
                    yield c, slice(at.start + i, at.start + i + 64), slice(inside.start + i, inside.start + i + 64)

        def fold(x):
            return x.reshape(-1, 8, x.shape[1])

        def products(window, cols):
            dp_scr[window, cols] = dot(sequence_ref[window, HEAD_DIM:], g_ref[cols, :], NT)
            scores = dot(sequence_ref[window, :HEAD_DIM], q_ref[cols, :], NT)
            peak8 = jnp.full((8, cols.stop - cols.start), neg_large, F32)
            for c, at, inside in tiles(window):
                allowed = offset[inside] >= first[:, cols] - c * row_count
                if c == here and inside.stop > cols.start // 2:
                    allowed = allowed & (offset[inside] <= last[:, cols])
                part = scores[at.start - window.start : at.stop - window.start]
                part = jnp.where(allowed, part, neg_large)
                w_scr[at, cols] = part
                peak8 = jnp.maximum(peak8, jnp.max(fold(part), axis=0))
            return jnp.max(peak8, axis=0, keepdims=True)

        def weigh(window, cols, peak):
            width = cols.stop - cols.start
            total8 = jnp.zeros((8, width), F32)
            mean8 = jnp.zeros((8, width), F32)
            for _, at, _ in tiles(window):
                w = jnp.exp2((w_scr[at, cols] - peak) * factor)
                w_scr[at, cols] = w
                total8 += jnp.sum(fold(w), axis=0)
                mean8 += jnp.sum(fold(w * dp_scr[at, cols]), axis=0)
            share = 1.0 / jnp.sum(total8, axis=0, keepdims=True)
            center = jnp.sum(mean8, axis=0, keepdims=True) * share
            for _, at, _ in tiles(window):
                p = w_scr[at, cols] * share
                low_ref[at, cols] = p.astype(BF16)
                ds_ref[at, cols] = (p * (dp_scr[at, cols] - center)).astype(BF16)

        def spread(window, cols, start):
            dv = dot(low_ref[window, cols], g_ref[cols, :])
            dk = dot(ds_ref[window, cols], q_ref[cols, :])
            old = slice(window.start, start)
            if start > window.start:
                dv_scr[old, :] += dv[: start - window.start]
                dk_scr[old, :] += dk[: start - window.start]
            dv_scr[start : window.stop, :] = dv[start - window.start :]
            dk_scr[start : window.stop, :] = dk[start - window.start :]

        start = blocks[0][0].start
        peak = products(*blocks[0])
        starts = [blocks[0][0].start] + [window.stop for window, _ in blocks]
        for b, (window, cols) in enumerate(blocks):
            after = products(*blocks[b + 1]) if b + 1 < len(blocks) else None
            if b:
                spread(*blocks[b - 1], starts[b - 1])
            weigh(window, cols, peak)
            peak = after
        spread(*blocks[-1], starts[len(blocks) - 1])
        for c in range(span):
            grad, half = ((own_grad_ref, 0), (far_grad_ref, 0), (own_grad_ref, 1), (far_grad_ref, 1))[here ^ c]
            to, at = slice(half * rows, (half + 1) * rows), slice(c * rows, (c + 1) * rows)
            if c <= here and at.stop > blocks[0][0].start:
                grad[to, HEAD_DIM:] = dv_scr[at, :].astype(BF16)
                grad[to, :HEAD_DIM] = (dk_scr[at, :] * score_scale).astype(BF16)
            else:
                grad[to, :] = jnp.zeros((rows, 2 * HEAD_DIM), BF16)

    for here in range(span):
        pl.when(shard == here)(functools.partial(attend, here))


def gather_kernel(peers, pad, row_count, span, sequence_ref, low_ref, ds_ref, *refs):
    out_refs, turned_scr, whole_scr = refs[:peers], refs[peers], refs[peers + 1]
    rows = peers * pad
    me = lax.axis_index("dp")
    shard = lax.axis_index("seq")

    def gather(here):
        blocks = windows(here, rows, pad, row_count)
        seen = slice(blocks[0][0].start, blocks[-1][0].stop)
        keys, values = sequence_ref[seen, :HEAD_DIM].T, sequence_ref[seen, HEAD_DIM:].T
        for window, cols in blocks:
            part = slice(window.start - seen.start, window.stop - seen.start)
            turned_scr[:HEAD_DIM, cols] = dot(values[:, part], low_ref[window, cols]).astype(BF16)
            dq = dot(keys[:, part], ds_ref[window, cols]) * score_scale
            turned_scr[HEAD_DIM:, cols] = dq.astype(BF16)

    for here in range(span):
        pl.when(shard == here)(functools.partial(gather, here))

    unit = math.gcd(pad, LANES)
    for column in range(2):
        whole_scr[...] = turned_scr[column * HEAD_DIM : (column + 1) * HEAD_DIM, :].T
        for p in range(peers):
            for t in range(pad // unit):
                for h in range(2):
                    at = pl.ds(stacked_row(step_to(p, me, peers) * pad + t * unit, h, unit), unit)
                    to = (2 * column + h) * HEAD_DIM
                    out_refs[p][t * unit : (t + 1) * unit, to : to + HEAD_DIM] = whole_scr[at, :]


def settle_kernel(peers, back_ref, *refs):
    pieces, outs = refs[:peers], refs[peers:]
    order = travel_order(peers)
    whole = jnp.concatenate([pieces[order.index(p)][...] for p in range(peers)], axis=0)
    settled = dot(back_ref[...], whole).astype(BF16)
    at = 0
    for out in outs:
        out[...] = settled[:, at : at + out.shape[1]]
        at += out.shape[1]


def join_kernel(peers, *refs):
    whole = refs[-1]
    pad = refs[0].shape[0]
    me = lax.axis_index("dp")
    for step, ref in zip(travel_order(peers), refs):
        whole[pl.ds(pl.multiple_of(step_to(step, me, peers) * pad, pad), pad), :] = ref[...]


def pair_kernel(peers, own_ref, returned_ref, after_ref, *outs):
    rows = own_ref.shape[0] // 2
    pad = rows // peers
    me = lax.axis_index("dp")
    for half in range(2):
        for step in range(peers):
            row = half * rows + step_to(step, me, peers) * pad
            at = pl.ds(pl.multiple_of(row, pad), pad)
            both = own_ref[at, :].astype(F32) + returned_ref[at, :].astype(F32)
            if half == 0:
                outs[0][step * pad : (step + 1) * pad, :] = both
            else:
                part, place = divmod(step * pad, outs[1].shape[0])
                outs[1 + part][place : place + pad, :] = both.astype(BF16)


def sum_kernel(parts, mine_ref, *refs):
    theirs, outs = refs[:parts], refs[parts + 1 :]
    pad = outs[0].shape[0]
    for step, out in enumerate(outs):
        part, place = divmod(step * pad, theirs[0].shape[0])
        out[...] = (
            mine_ref[step * pad : (step + 1) * pad, :]
            + theirs[part][place : place + pad, :].astype(F32)
        ).astype(BF16)


def call(kernel, outs, *args, scratch=(), in_specs=None, cost=None):
    return pl.pallas_call(
        kernel,
        out_shape=outs,
        in_specs=in_specs or [pl.BlockSpec(memory_space=pltpu.VMEM)] * len(args),
        scratch_shapes=scratch,
        compiler_params=pltpu.CompilerParams(vmem_limit_bytes=vmem_bytes),
        cost_estimate=cost,
    )(*args)


def local(queries, key_rows, value_rows, grad_out, doc_lengths, dest_index):
    row_count = queries.shape[1]
    peers = lax.axis_size("dp")
    span = lax.axis_size("seq")
    group_rows = row_count // peers
    pad = -(-group_rows // TILE) * TILE
    rows = peers * pad
    shape = jax.ShapeDtypeStruct

    sources = [
        pltpu.with_memory_space_constraint(a, pltpu.HBM)
        for a in (doc_lengths, dest_index, queries[0], key_rows[0], value_rows[0], grad_out[0])
    ]
    lengths, dest, q, k, v, g = sources
    *kv, slot, first_seen, q, g = call(
        functools.partial(sort_kernel, peers, pad),
        [shape((pad, 2 * HEAD_DIM), BF16)] * peers
        + [shape((1, row_count), jnp.int32), shape((1, 2 * rows), jnp.int32)]
        + [shape(q.shape, BF16)] * 2,
        lengths,
        dest,
        k,
        v,
        q,
        g,
        in_specs=[pl.BlockSpec(memory_space=pltpu.HBM)] * 6,
        scratch=[pltpu.SMEM(lengths.shape, jnp.int32), pltpu.VMEM(dest.shape, jnp.int32)]
        + [pltpu.VMEM((row_count, 2 * HEAD_DIM), BF16)]
        + [pltpu.SemaphoreType.DMA((6,))],
    )
    qg = call(
        functools.partial(follow_kernel, peers, pad),
        [shape((pad, 4 * HEAD_DIM), BF16)] * peers,
        slot,
        q,
        g,
        cost=pause,
    )

    def exchange(pieces, home=False, order=travel_order(peers)):
        arrived = []
        for k in order:
            way = [(i, receiver_of(i, k, peers)) for i in range(peers)]
            if home:
                way = [(j, i) for i, j in way]
            arrived.append(lax.ppermute(pieces[k], "dp", way) if k else pieces[k])
        return arrived

    def to_partner(values, distance):
        return lax.ppermute(values, "seq", [(i, i ^ distance) for i in range(span)])

    def join(pieces):
        return call(functools.partial(join_kernel, peers), shape((rows, 2 * HEAD_DIM), BF16), *pieces, cost=brief)

    kv = exchange(kv)
    near_first = [1, *range(peers - 1, 1, -1), 0]
    qg = exchange(qg, order=near_first)
    sequence = lax.all_gather(join(kv), "seq", axis=0, tiled=True)
    back = call(back_kernel, shape((row_count, rows), BF16), slot)

    wide = (span * rows, 2 * rows)
    own_grad, far_grad, low, ds = call(
        functools.partial(attend_kernel, near_first, pad, row_count, span),
        [shape((2 * rows, 2 * HEAD_DIM), BF16)] * 2 + [shape(wide, BF16)] * 2,
        sequence,
        first_seen,
        *qg,
        scratch=[pltpu.VMEM(wide, F32)] * 2
        + [pltpu.VMEM((span * rows, HEAD_DIM), F32)] * 2
        + [pltpu.VMEM((2 * rows, HEAD_DIM), BF16)] * 2,
    )
    attended = call(
        functools.partial(gather_kernel, peers, pad, row_count, span),
        [shape((pad, 4 * HEAD_DIM), BF16)] * peers,
        sequence,
        low,
        ds,
        scratch=[pltpu.VMEM((2 * HEAD_DIM, 2 * rows), BF16), pltpu.VMEM((2 * rows, HEAD_DIM), BF16)],
    )

    returned = to_partner(far_grad, 1)
    parts = PARTS
    mine, *theirs = call(
        functools.partial(pair_kernel, peers),
        [shape((rows, 2 * HEAD_DIM), F32)] + [shape((rows // parts, 2 * HEAD_DIM), BF16)] * parts,
        own_grad,
        returned,
        attended[0],
        cost=pause,
    )
    attended = exchange(attended, home=True)
    pair_grad = call(
        functools.partial(sum_kernel, parts),
        [shape((pad, 2 * HEAD_DIM), BF16)] * peers,
        mine,
        *[to_partner(part, 2) for part in theirs],
        attended[0],
        cost=pause,
    )
    pair_grad = exchange(pair_grad, home=True)

    wide, narrow = shape((row_count, 2 * HEAD_DIM), BF16), shape((row_count, HEAD_DIM), BF16)
    first = call(
        functools.partial(settle_kernel, peers), [wide, wide], back, *attended
    )
    last = call(functools.partial(settle_kernel, peers), [narrow, narrow], back, *pair_grad)
    return first[0][None], first[1][None], last[0][None], last[1][None]


def solution(mesh):
    split = P("dp", "seq", "head")
    return jax.shard_map(
        local,
        mesh=mesh,
        in_specs=(split, split, split, split, P("dp", None), P("dp", "seq")),
        out_specs=(split, split, split, split),
        check_vma=False,
    )
```

```python
import functools
import math

import jax
import jax.numpy as jnp
from jax import lax
from jax.experimental import pallas as pl
from jax.experimental.pallas import tpu as pltpu
from jax.sharding import PartitionSpec as P

HEAD_DIM = 128
WINDOW = 1024
TILE = 16
LANES = 128
PARTS = 2

score_scale = 168.0 ** (-0.5)
log2_e = 1.4426950408889634
neg_large = -1e30
vmem_bytes = 24 * 1024 * 1024
brief = pl.CostEstimate(flops=1, bytes_accessed=1, transcendentals=0)
pause = pl.CostEstimate(flops=10**11, bytes_accessed=10**8, transcendentals=0)

F32 = jnp.float32
BF16 = jnp.bfloat16
NT = (((1,), (1,)), ((), ()))
TN = (((0,), (0,)), ((), ()))


def dot(a, b, dims=(((1,), (0,)), ((), ()))):
    return lax.dot_general(a, b, dims, preferred_element_type=F32)


def receiver_of(me, step, peers):
    return me ^ step if peers & (peers - 1) == 0 else (me + step) % peers


def travel_order(peers):
    return list(range(2, peers)) + [1, 0]


def far_first(peers):
    return list(range(peers))[::-1]


def step_to(me, other, peers):
    if peers & (peers - 1) == 0:
        return other ^ me
    step = other - me
    return jnp.where(step < 0, step + peers, step)


def position_of(row, pad, group_rows):
    group, inner = row // pad, row % pad
    last = group_rows - 1
    return group * group_rows + (min(inner, last) if isinstance(row, int) else jnp.minimum(inner, last)), inner


def query_positions(rows, pad, row_count):
    lane = lax.broadcasted_iota(jnp.int32, (1, 2 * rows), 1)
    row = lane // (2 * LANES) * LANES + lane % LANES
    return position_of(row, pad, row_count * pad // rows)[0]


def stacked_row(row, head, unit):
    return pl.multiple_of(row // LANES * (2 * LANES) + head * LANES + row % LANES, unit)


def place_of(slot, slots):
    here = lax.broadcasted_iota(jnp.int32, (slots, slot.shape[1]), 0) == slot
    return here.astype(F32).astype(BF16)


def sort_kernel(peers, pad, lengths_hbm, dest_hbm, k_hbm, v_hbm, q_hbm, g_hbm, *refs):
    outs, slot_ref, first_ref, q_ref, g_ref = refs[:peers], *refs[peers : peers + 4]
    lengths_ref, dest_ref, kv_ref, sems = refs[peers + 4 :]
    loads = (
        (dest_hbm, dest_ref),
        (k_hbm, kv_ref.at[:, :HEAD_DIM]),
        (v_hbm, kv_ref.at[:, HEAD_DIM:]),
        (lengths_hbm, lengths_ref),
        (q_hbm, q_ref),
        (g_hbm, g_ref),
    )
    copies = [pltpu.make_async_copy(*pair, sems.at[i]) for i, pair in enumerate(loads)]
    for copy in copies:
        copy.start()
    rows = kv_ref.shape[0]
    me = lax.axis_index("dp")
    wide = -(-peers // TILE) * TILE
    lane = lax.broadcasted_iota(jnp.int32, (wide, rows), 0)
    upto = (
        lax.broadcasted_iota(jnp.int32, (rows, rows), 0)
        <= lax.broadcasted_iota(jnp.int32, (rows, rows), 1)
    ).astype(F32)
    copies[0].wait()
    member = (lane == step_to(me, dest_ref[...], peers)).astype(F32)
    count = dot(member.astype(BF16), upto.astype(BF16))
    slot = jnp.sum(member * (count + (lane * pad - 1).astype(F32)), axis=0, keepdims=True)
    slot = slot.astype(jnp.int32)
    slot_ref[...] = slot
    place = place_of(slot, peers * pad)
    for copy in copies[1:3]:
        copy.wait()
    moved = dot(place, kv_ref[...]).astype(BF16)
    for p in range(peers):
        outs[p][...] = moved[p * pad : (p + 1) * pad]
    copies[3].wait()
    query_pos = query_positions(peers * pad, pad, rows) + lax.axis_index("seq") * rows
    first = jnp.maximum(query_pos - (WINDOW - 1), 0)
    edge = jnp.int32(0)
    for e in range(lengths_ref.shape[1]):
        edge = edge + lengths_ref[0, e]
        first = jnp.maximum(first, jnp.where(edge <= query_pos, edge, 0))
    first_ref[...] = first
    for copy in copies[4:]:
        copy.wait()


def follow_kernel(peers, pad, slot_ref, q_ref, g_ref, *outs):
    place = place_of(slot_ref[...], peers * pad)
    for ref, at in ((q_ref, 0), (g_ref, 2)):
        moved = dot(place, ref[...]).astype(BF16)
        for p in range(peers):
            outs[p][:, at * HEAD_DIM : (at + 2) * HEAD_DIM] = moved[p * pad : (p + 1) * pad]


def back_kernel(slot_ref, back_ref):
    rows, slots = back_ref.shape
    slot = slot_ref[...]
    eye = lax.broadcasted_iota(jnp.int32, (rows, rows), 0) == lax.broadcasted_iota(
        jnp.int32, (rows, rows), 1
    )
    column = jnp.sum(jnp.where(eye, slot, 0), axis=1, keepdims=True)
    back_ref[...] = (
        (lax.broadcasted_iota(jnp.int32, (rows, slots), 1) == column).astype(F32).astype(BF16)
    )


def windows(here, rows, pad, row_count):
    group_rows = row_count // (rows // pad)
    blocks = []
    for b in range(rows // LANES):
        reach = here * row_count + position_of(b * LANES, pad, group_rows)[0] - (WINDOW - 1)
        reach = max(reach, 0)
        row = reach // row_count * rows + reach % row_count // group_rows * pad + reach % group_rows
        keys = slice(row // LANES * LANES, here * rows + (b + 1) * LANES)
        blocks.append((keys, slice(2 * b * LANES, 2 * (b + 1) * LANES)))
    return blocks


def stack(order, pieces, stacks):
    peers = len(order)
    pad = pieces[0].shape[0]
    unit = math.gcd(pad, LANES)
    me = lax.axis_index("dp")
    for step, piece in zip(order, pieces):
        for t in range(pad // unit):
            for h in range(2):
                to = pl.ds(stacked_row(step_to(step, me, peers) * pad + t * unit, h, unit), unit)
                for column, out in enumerate(stacks):
                    at = (2 * column + h) * HEAD_DIM
                    out[to, :] = piece[t * unit : (t + 1) * unit, at : at + HEAD_DIM]


def attend_kernel(order, pad, row_count, span, sequence_ref, first_ref, *refs):
    peers = len(order)
    own_grad_ref, far_grad_ref, low_ref, ds_ref = refs[peers : peers + 4]
    w_scr, dp_scr, dv_scr, dk_scr, q_ref, g_ref = refs[peers + 4 :]
    stack(order, refs[:peers], (q_ref, g_ref))
    rows = peers * pad
    shard = lax.axis_index("seq")
    factor = score_scale * log2_e
    first, last = first_ref[...], query_positions(rows, pad, row_count)
    group_rows = row_count // peers
    offset, inner = position_of(lax.broadcasted_iota(jnp.int32, (rows, 1), 0), pad, group_rows)
    offset = jnp.where(inner < group_rows, offset, -(2**24))

    def attend(here):
        blocks = windows(here, rows, pad, row_count)

        def strips(window):
            at = window.start
            while at < window.stop:
                end = min(at - at % rows + rows, window.stop)
                yield at // rows, slice(at, end), slice(at % rows, at % rows + end - at)
                at = end

        def tiles(window):
            for c, at, inside in strips(window):
                for i in range(0, at.stop - at.start, 64):
                    yield c, slice(at.start + i, at.start + i + 64), slice(inside.start + i, inside.start + i + 64)

        def fold(x):
            return x.reshape(-1, 8, x.shape[1])

        def products(window, cols):
            dp_scr[window, cols] = dot(sequence_ref[window, HEAD_DIM:], g_ref[cols, :], NT)
            scores = dot(sequence_ref[window, :HEAD_DIM], q_ref[cols, :], NT)
            peak8 = jnp.full((8, cols.stop - cols.start), neg_large, F32)
            for c, at, inside in tiles(window):
                allowed = offset[inside] >= first[:, cols] - c * row_count
                if c == here and inside.stop > cols.start // 2:
                    allowed = allowed & (offset[inside] <= last[:, cols])
                part = scores[at.start - window.start : at.stop - window.start]
                part = jnp.where(allowed, part, neg_large)
                w_scr[at, cols] = part
                peak8 = jnp.maximum(peak8, jnp.max(fold(part), axis=0))
            return jnp.max(peak8, axis=0, keepdims=True)

        def weigh(window, cols, peak):
            width = cols.stop - cols.start
            total8 = jnp.zeros((8, width), F32)
            mean8 = jnp.zeros((8, width), F32)
            for _, at, _ in tiles(window):
                w = jnp.exp2((w_scr[at, cols] - peak) * factor)
                w_scr[at, cols] = w
                total8 += jnp.sum(fold(w), axis=0)
                mean8 += jnp.sum(fold(w * dp_scr[at, cols]), axis=0)
            share = 1.0 / jnp.sum(total8, axis=0, keepdims=True)
            center = jnp.sum(mean8, axis=0, keepdims=True) * share
            for _, at, _ in tiles(window):
                p = w_scr[at, cols] * share
                low_ref[at, cols] = p.astype(BF16)
                ds_ref[at, cols] = (p * (dp_scr[at, cols] - center)).astype(BF16)

        def spread(window, cols, start):
            dv = dot(low_ref[window, cols], g_ref[cols, :])
            dk = dot(ds_ref[window, cols], q_ref[cols, :])
            old = slice(window.start, start)
            if start > window.start:
                dv_scr[old, :] += dv[: start - window.start]
                dk_scr[old, :] += dk[: start - window.start]
            dv_scr[start : window.stop, :] = dv[start - window.start :]
            dk_scr[start : window.stop, :] = dk[start - window.start :]

        start = blocks[0][0].start
        peak = products(*blocks[0])
        starts = [blocks[0][0].start] + [window.stop for window, _ in blocks]
        for b, (window, cols) in enumerate(blocks):
            after = products(*blocks[b + 1]) if b + 1 < len(blocks) else None
            if b:
                spread(*blocks[b - 1], starts[b - 1])
            weigh(window, cols, peak)
            peak = after
        spread(*blocks[-1], starts[len(blocks) - 1])
        for c in range(span):
            grad, half = ((own_grad_ref, 0), (far_grad_ref, 0), (own_grad_ref, 1), (far_grad_ref, 1))[here ^ c]
            to, at = slice(half * rows, (half + 1) * rows), slice(c * rows, (c + 1) * rows)
            if c <= here and at.stop > blocks[0][0].start:
                grad[to, HEAD_DIM:] = dv_scr[at, :].astype(BF16)
                grad[to, :HEAD_DIM] = (dk_scr[at, :] * score_scale).astype(BF16)
            else:
                grad[to, :] = jnp.zeros((rows, 2 * HEAD_DIM), BF16)

    for here in range(span):
        pl.when(shard == here)(functools.partial(attend, here))


def gather_kernel(peers, pad, row_count, span, sequence_ref, low_ref, ds_ref, *refs):
    out_refs, turned_scr, whole_scr = refs[:peers], refs[peers], refs[peers + 1]
    rows = peers * pad
    me = lax.axis_index("dp")
    shard = lax.axis_index("seq")

    def gather(here):
        blocks = windows(here, rows, pad, row_count)
        seen = slice(blocks[0][0].start, blocks[-1][0].stop)
        keys, values = sequence_ref[seen, :HEAD_DIM].T, sequence_ref[seen, HEAD_DIM:].T
        for window, cols in blocks:
            part = slice(window.start - seen.start, window.stop - seen.start)
            turned_scr[:HEAD_DIM, cols] = dot(values[:, part], low_ref[window, cols]).astype(BF16)
            dq = dot(keys[:, part], ds_ref[window, cols]) * score_scale
            turned_scr[HEAD_DIM:, cols] = dq.astype(BF16)

    for here in range(span):
        pl.when(shard == here)(functools.partial(gather, here))

    unit = math.gcd(pad, LANES)
    for column in range(2):
        whole_scr[...] = turned_scr[column * HEAD_DIM : (column + 1) * HEAD_DIM, :].T
        for p in range(peers):
            for t in range(pad // unit):
                for h in range(2):
                    at = pl.ds(stacked_row(step_to(p, me, peers) * pad + t * unit, h, unit), unit)
                    to = (2 * column + h) * HEAD_DIM
                    out_refs[p][t * unit : (t + 1) * unit, to : to + HEAD_DIM] = whole_scr[at, :]


def settle_kernel(peers, back_ref, *refs):
    pieces, outs = refs[:peers], refs[peers:]
    order = travel_order(peers)
    whole = jnp.concatenate([pieces[order.index(p)][...] for p in range(peers)], axis=0)
    settled = dot(back_ref[...], whole).astype(BF16)
    at = 0
    for out in outs:
        out[...] = settled[:, at : at + out.shape[1]]
        at += out.shape[1]


def join_kernel(peers, *refs):
    whole = refs[-1]
    pad = refs[0].shape[0]
    me = lax.axis_index("dp")
    for step, ref in zip(far_first(peers), refs):
        whole[pl.ds(pl.multiple_of(step_to(step, me, peers) * pad, pad), pad), :] = ref[...]


def pair_kernel(peers, own_ref, returned_ref, after_ref, *outs):
    rows = own_ref.shape[0] // 2
    pad = rows // peers
    me = lax.axis_index("dp")
    for half in range(2):
        for step in range(peers):
            row = half * rows + step_to(step, me, peers) * pad
            at = pl.ds(pl.multiple_of(row, pad), pad)
            both = own_ref[at, :].astype(F32) + returned_ref[at, :].astype(F32)
            if half == 0:
                outs[0][step * pad : (step + 1) * pad, :] = both
            else:
                part, place = divmod(step * pad, outs[1].shape[0])
                outs[1 + part][place : place + pad, :] = both.astype(BF16)


def sum_kernel(parts, mine_ref, *refs):
    theirs, outs = refs[:parts], refs[parts + 1 :]
    pad = outs[0].shape[0]
    for step, out in enumerate(outs):
        part, place = divmod(step * pad, theirs[0].shape[0])
        out[...] = (
            mine_ref[step * pad : (step + 1) * pad, :]
            + theirs[part][place : place + pad, :].astype(F32)
        ).astype(BF16)


def call(kernel, outs, *args, scratch=(), in_specs=None, cost=None):
    return pl.pallas_call(
        kernel,
        out_shape=outs,
        in_specs=in_specs or [pl.BlockSpec(memory_space=pltpu.VMEM)] * len(args),
        scratch_shapes=scratch,
        compiler_params=pltpu.CompilerParams(vmem_limit_bytes=vmem_bytes),
        cost_estimate=cost,
    )(*args)


def local(queries, key_rows, value_rows, grad_out, doc_lengths, dest_index):
    row_count = queries.shape[1]
    peers = lax.axis_size("dp")
    span = lax.axis_size("seq")
    group_rows = row_count // peers
    pad = -(-group_rows // TILE) * TILE
    rows = peers * pad
    shape = jax.ShapeDtypeStruct

    sources = [
        pltpu.with_memory_space_constraint(a, pltpu.HBM)
        for a in (doc_lengths, dest_index, queries[0], key_rows[0], value_rows[0], grad_out[0])
    ]
    lengths, dest, q, k, v, g = sources
    *kv, slot, first_seen, q, g = call(
        functools.partial(sort_kernel, peers, pad),
        [shape((pad, 2 * HEAD_DIM), BF16)] * peers
        + [shape((1, row_count), jnp.int32), shape((1, 2 * rows), jnp.int32)]
        + [shape(q.shape, BF16)] * 2,
        lengths,
        dest,
        k,
        v,
        q,
        g,
        in_specs=[pl.BlockSpec(memory_space=pltpu.HBM)] * 6,
        scratch=[pltpu.SMEM(lengths.shape, jnp.int32), pltpu.VMEM(dest.shape, jnp.int32)]
        + [pltpu.VMEM((row_count, 2 * HEAD_DIM), BF16)]
        + [pltpu.SemaphoreType.DMA((6,))],
    )
    qg = call(
        functools.partial(follow_kernel, peers, pad),
        [shape((pad, 4 * HEAD_DIM), BF16)] * peers,
        slot,
        q,
        g,
        cost=pause,
    )

    def exchange(pieces, home=False, order=travel_order(peers)):
        arrived = []
        for k in order:
            way = [(i, receiver_of(i, k, peers)) for i in range(peers)]
            if home:
                way = [(j, i) for i, j in way]
            arrived.append(lax.ppermute(pieces[k], "dp", way) if k else pieces[k])
        return arrived

    def to_partner(values, distance):
        return lax.ppermute(values, "seq", [(i, i ^ distance) for i in range(span)])

    def join(pieces):
        return call(functools.partial(join_kernel, peers), shape((rows, 2 * HEAD_DIM), BF16), *pieces, cost=brief)

    kv = exchange(kv, order=far_first(peers))
    near_first = [1, *range(peers - 1, 1, -1), 0]
    qg = exchange(qg, order=near_first)
    sequence = lax.all_gather(join(kv), "seq", axis=0, tiled=True)
    back = call(back_kernel, shape((row_count, rows), BF16), slot)

    wide = (span * rows, 2 * rows)
    own_grad, far_grad, low, ds = call(
        functools.partial(attend_kernel, near_first, pad, row_count, span),
        [shape((2 * rows, 2 * HEAD_DIM), BF16)] * 2 + [shape(wide, BF16)] * 2,
        sequence,
        first_seen,
        *qg,
        scratch=[pltpu.VMEM(wide, F32)] * 2
        + [pltpu.VMEM((span * rows, HEAD_DIM), F32)] * 2
        + [pltpu.VMEM((2 * rows, HEAD_DIM), BF16)] * 2,
    )
    attended = call(
        functools.partial(gather_kernel, peers, pad, row_count, span),
        [shape((pad, 4 * HEAD_DIM), BF16)] * peers,
        sequence,
        low,
        ds,
        scratch=[pltpu.VMEM((2 * HEAD_DIM, 2 * rows), BF16), pltpu.VMEM((2 * rows, HEAD_DIM), BF16)],
    )

    returned = to_partner(far_grad, 1)
    parts = PARTS
    mine, *theirs = call(
        functools.partial(pair_kernel, peers),
        [shape((rows, 2 * HEAD_DIM), F32)] + [shape((rows // parts, 2 * HEAD_DIM), BF16)] * parts,
        own_grad,
        returned,
        attended[0],
        cost=pause,
    )
    attended = exchange(attended, home=True)
    pair_grad = call(
        functools.partial(sum_kernel, parts),
        [shape((pad, 2 * HEAD_DIM), BF16)] * peers,
        mine,
        *[to_partner(part, 2) for part in theirs],
        attended[0],
        cost=pause,
    )
    pair_grad = exchange(pair_grad, home=True)

    wide, narrow = shape((row_count, 2 * HEAD_DIM), BF16), shape((row_count, HEAD_DIM), BF16)
    first = call(
        functools.partial(settle_kernel, peers), [wide, wide], back, *attended
    )
    last = call(functools.partial(settle_kernel, peers), [narrow, narrow], back, *pair_grad)
    return first[0][None], first[1][None], last[0][None], last[1][None]


def solution(mesh):
    split = P("dp", "seq", "head")
    return jax.shard_map(
        local,
        mesh=mesh,
        in_specs=(split, split, split, split, P("dp", None), P("dp", "seq")),
        out_specs=(split, split, split, split),
        check_vma=False,
    )
```

```python
import functools
import math

import jax
import jax.numpy as jnp
from jax import lax
from jax.experimental import pallas as pl
from jax.experimental.pallas import tpu as pltpu
from jax.sharding import PartitionSpec as P

HEAD_DIM = 128
WINDOW = 1024
TILE = 16
LANES = 128
PARTS = 2

score_scale = 168.0 ** (-0.5)
log2_e = 1.4426950408889634
neg_large = -1e30
vmem_bytes = 24 * 1024 * 1024
brief = pl.CostEstimate(flops=1, bytes_accessed=1, transcendentals=0)
pause = pl.CostEstimate(flops=10**11, bytes_accessed=10**8, transcendentals=0)

F32 = jnp.float32
BF16 = jnp.bfloat16
NT = (((1,), (1,)), ((), ()))
TN = (((0,), (0,)), ((), ()))


def dot(a, b, dims=(((1,), (0,)), ((), ()))):
    return lax.dot_general(a, b, dims, preferred_element_type=F32)


def receiver_of(me, step, peers):
    return me ^ step if peers & (peers - 1) == 0 else (me + step) % peers


def travel_order(peers):
    return list(range(2, peers)) + [1, 0]


def far_first(peers):
    return list(range(peers))[::-1]


def step_to(me, other, peers):
    if peers & (peers - 1) == 0:
        return other ^ me
    step = other - me
    return jnp.where(step < 0, step + peers, step)


def position_of(row, pad, group_rows):
    group, inner = row // pad, row % pad
    last = group_rows - 1
    return group * group_rows + (min(inner, last) if isinstance(row, int) else jnp.minimum(inner, last)), inner


def query_positions(rows, pad, row_count):
    lane = lax.broadcasted_iota(jnp.int32, (1, 2 * rows), 1)
    row = lane // (2 * LANES) * LANES + lane % LANES
    return position_of(row, pad, row_count * pad // rows)[0]


def stacked_row(row, head, unit):
    return pl.multiple_of(row // LANES * (2 * LANES) + head * LANES + row % LANES, unit)


def place_of(slot, slots):
    here = lax.broadcasted_iota(jnp.int32, (slots, slot.shape[1]), 0) == slot
    return here.astype(F32).astype(BF16)


def sort_kernel(peers, pad, lengths_hbm, dest_hbm, k_hbm, v_hbm, q_hbm, g_hbm, *refs):
    outs, slot_ref, first_ref, q_ref, g_ref = refs[:peers], *refs[peers : peers + 4]
    lengths_ref, dest_ref, kv_ref, sems = refs[peers + 4 :]
    loads = (
        (dest_hbm, dest_ref),
        (k_hbm, kv_ref.at[:, :HEAD_DIM]),
        (v_hbm, kv_ref.at[:, HEAD_DIM:]),
        (lengths_hbm, lengths_ref),
        (q_hbm, q_ref),
        (g_hbm, g_ref),
    )
    copies = [pltpu.make_async_copy(*pair, sems.at[i]) for i, pair in enumerate(loads)]
    for copy in copies:
        copy.start()
    rows = kv_ref.shape[0]
    me = lax.axis_index("dp")
    wide = -(-peers // TILE) * TILE
    lane = lax.broadcasted_iota(jnp.int32, (wide, rows), 0)
    upto = (
        lax.broadcasted_iota(jnp.int32, (rows, rows), 0)
        <= lax.broadcasted_iota(jnp.int32, (rows, rows), 1)
    ).astype(F32)
    copies[0].wait()
    member = (lane == step_to(me, dest_ref[...], peers)).astype(F32)
    count = dot(member.astype(BF16), upto.astype(BF16))
    slot = jnp.sum(member * (count + (lane * pad - 1).astype(F32)), axis=0, keepdims=True)
    slot = slot.astype(jnp.int32)
    slot_ref[...] = slot
    place = place_of(slot, peers * pad)
    for copy in copies[1:3]:
        copy.wait()
    moved = dot(place, kv_ref[...]).astype(BF16)
    for p in range(peers):
        outs[p][...] = moved[p * pad : (p + 1) * pad]
    copies[3].wait()
    query_pos = query_positions(peers * pad, pad, rows) + lax.axis_index("seq") * rows
    first = jnp.maximum(query_pos - (WINDOW - 1), 0)
    edge = jnp.int32(0)
    for e in range(lengths_ref.shape[1]):
        edge = edge + lengths_ref[0, e]
        first = jnp.maximum(first, jnp.where(edge <= query_pos, edge, 0))
    first_ref[...] = first
    for copy in copies[4:]:
        copy.wait()


def follow_kernel(peers, pad, slot_ref, q_ref, g_ref, *outs):
    place = place_of(slot_ref[...], peers * pad)
    for ref, at in ((q_ref, 0), (g_ref, 2)):
        moved = dot(place, ref[...]).astype(BF16)
        for p in range(peers):
            outs[p][:, at * HEAD_DIM : (at + 2) * HEAD_DIM] = moved[p * pad : (p + 1) * pad]


def back_kernel(slot_ref, back_ref):
    rows, slots = back_ref.shape
    slot = slot_ref[...]
    eye = lax.broadcasted_iota(jnp.int32, (rows, rows), 0) == lax.broadcasted_iota(
        jnp.int32, (rows, rows), 1
    )
    column = jnp.sum(jnp.where(eye, slot, 0), axis=1, keepdims=True)
    back_ref[...] = (
        (lax.broadcasted_iota(jnp.int32, (rows, slots), 1) == column).astype(F32).astype(BF16)
    )


def windows(here, rows, pad, row_count):
    group_rows = row_count // (rows // pad)
    blocks = []
    for b in range(rows // LANES):
        reach = here * row_count + position_of(b * LANES, pad, group_rows)[0] - (WINDOW - 1)
        reach = max(reach, 0)
        row = reach // row_count * rows + reach % row_count // group_rows * pad + reach % group_rows
        keys = slice(row // LANES * LANES, here * rows + (b + 1) * LANES)
        blocks.append((keys, slice(2 * b * LANES, 2 * (b + 1) * LANES)))
    return blocks


def stack(order, pieces, stacks):
    peers = len(order)
    pad = pieces[0].shape[0]
    unit = math.gcd(pad, LANES)
    me = lax.axis_index("dp")
    for step, piece in zip(order, pieces):
        for t in range(pad // unit):
            for h in range(2):
                to = pl.ds(stacked_row(step_to(step, me, peers) * pad + t * unit, h, unit), unit)
                for column, out in enumerate(stacks):
                    at = (2 * column + h) * HEAD_DIM
                    out[to, :] = piece[t * unit : (t + 1) * unit, at : at + HEAD_DIM]


def attend_kernel(order, pad, row_count, span, sequence_ref, first_ref, *refs):
    peers = len(order)
    own_grad_ref, far_grad_ref, low_ref, ds_ref = refs[peers : peers + 4]
    w_scr, dp_scr, dv_scr, dk_scr, q_ref, g_ref = refs[peers + 4 :]
    stack(order, refs[:peers], (q_ref, g_ref))
    rows = peers * pad
    shard = lax.axis_index("seq")
    factor = score_scale * log2_e
    first, last = first_ref[...], query_positions(rows, pad, row_count)
    group_rows = row_count // peers
    offset, inner = position_of(lax.broadcasted_iota(jnp.int32, (rows, 1), 0), pad, group_rows)
    offset = jnp.where(inner < group_rows, offset, -(2**24))

    def attend(here):
        blocks = windows(here, rows, pad, row_count)

        def strips(window):
            at = window.start
            while at < window.stop:
                end = min(at - at % rows + rows, window.stop)
                yield at // rows, slice(at, end), slice(at % rows, at % rows + end - at)
                at = end

        def tiles(window):
            for c, at, inside in strips(window):
                for i in range(0, at.stop - at.start, 128):
                    yield c, slice(at.start + i, at.start + i + 128), slice(inside.start + i, inside.start + i + 128)

        def fold(x):
            return x.reshape(-1, 8, x.shape[1])

        def products(window, cols):
            dp_scr[window, cols] = dot(sequence_ref[window, HEAD_DIM:], g_ref[cols, :], NT)
            scores = dot(sequence_ref[window, :HEAD_DIM], q_ref[cols, :], NT)
            peak8 = jnp.full((8, cols.stop - cols.start), neg_large, F32)
            for c, at, inside in tiles(window):
                allowed = offset[inside] >= first[:, cols] - c * row_count
                if c == here and inside.stop > cols.start // 2:
                    allowed = allowed & (offset[inside] <= last[:, cols])
                part = scores[at.start - window.start : at.stop - window.start]
                part = jnp.where(allowed, part, neg_large)
                w_scr[at, cols] = part
                peak8 = jnp.maximum(peak8, jnp.max(fold(part), axis=0))
            return jnp.max(peak8, axis=0, keepdims=True)

        def weigh(window, cols, peak):
            width = cols.stop - cols.start
            total8 = jnp.zeros((8, width), F32)
            mean8 = jnp.zeros((8, width), F32)
            for _, at, _ in tiles(window):
                w = jnp.exp2((w_scr[at, cols] - peak) * factor)
                w_scr[at, cols] = w
                total8 += jnp.sum(fold(w), axis=0)
                mean8 += jnp.sum(fold(w * dp_scr[at, cols]), axis=0)
            share = 1.0 / jnp.sum(total8, axis=0, keepdims=True)
            center = jnp.sum(mean8, axis=0, keepdims=True) * share
            for _, at, _ in tiles(window):
                p = w_scr[at, cols] * share
                low_ref[at, cols] = p.astype(BF16)
                ds_ref[at, cols] = (p * (dp_scr[at, cols] - center)).astype(BF16)

        def spread(window, cols, start):
            dv = dot(low_ref[window, cols], g_ref[cols, :])
            dk = dot(ds_ref[window, cols], q_ref[cols, :])
            old = slice(window.start, start)
            if start > window.start:
                dv_scr[old, :] += dv[: start - window.start]
                dk_scr[old, :] += dk[: start - window.start]
            dv_scr[start : window.stop, :] = dv[start - window.start :]
            dk_scr[start : window.stop, :] = dk[start - window.start :]

        start = blocks[0][0].start
        peak = products(*blocks[0])
        starts = [blocks[0][0].start] + [window.stop for window, _ in blocks]
        for b, (window, cols) in enumerate(blocks):
            after = products(*blocks[b + 1]) if b + 1 < len(blocks) else None
            if b:
                spread(*blocks[b - 1], starts[b - 1])
            weigh(window, cols, peak)
            peak = after
        spread(*blocks[-1], starts[len(blocks) - 1])
        for c in range(span):
            grad, half = ((own_grad_ref, 0), (far_grad_ref, 0), (own_grad_ref, 1), (far_grad_ref, 1))[here ^ c]
            to, at = slice(half * rows, (half + 1) * rows), slice(c * rows, (c + 1) * rows)
            if c <= here and at.stop > blocks[0][0].start:
                grad[to, HEAD_DIM:] = dv_scr[at, :].astype(BF16)
                grad[to, :HEAD_DIM] = (dk_scr[at, :] * score_scale).astype(BF16)
            else:
                grad[to, :] = jnp.zeros((rows, 2 * HEAD_DIM), BF16)

    for here in range(span):
        pl.when(shard == here)(functools.partial(attend, here))


def gather_kernel(peers, pad, row_count, span, sequence_ref, low_ref, ds_ref, *refs):
    out_refs, turned_scr, whole_scr = refs[:peers], refs[peers], refs[peers + 1]
    rows = peers * pad
    me = lax.axis_index("dp")
    shard = lax.axis_index("seq")

    def gather(here):
        blocks = windows(here, rows, pad, row_count)
        seen = slice(blocks[0][0].start, blocks[-1][0].stop)
        keys, values = sequence_ref[seen, :HEAD_DIM].T, sequence_ref[seen, HEAD_DIM:].T
        for window, cols in blocks:
            part = slice(window.start - seen.start, window.stop - seen.start)
            turned_scr[:HEAD_DIM, cols] = dot(values[:, part], low_ref[window, cols]).astype(BF16)
            dq = dot(keys[:, part], ds_ref[window, cols]) * score_scale
            turned_scr[HEAD_DIM:, cols] = dq.astype(BF16)

    for here in range(span):
        pl.when(shard == here)(functools.partial(gather, here))

    unit = math.gcd(pad, LANES)
    for column in range(2):
        whole_scr[...] = turned_scr[column * HEAD_DIM : (column + 1) * HEAD_DIM, :].T
        for p in range(peers):
            for t in range(pad // unit):
                for h in range(2):
                    at = pl.ds(stacked_row(step_to(p, me, peers) * pad + t * unit, h, unit), unit)
                    to = (2 * column + h) * HEAD_DIM
                    out_refs[p][t * unit : (t + 1) * unit, to : to + HEAD_DIM] = whole_scr[at, :]


def settle_kernel(peers, back_ref, *refs):
    pieces, outs = refs[:peers], refs[peers:]
    order = travel_order(peers)
    whole = jnp.concatenate([pieces[order.index(p)][...] for p in range(peers)], axis=0)
    settled = dot(back_ref[...], whole).astype(BF16)
    at = 0
    for out in outs:
        out[...] = settled[:, at : at + out.shape[1]]
        at += out.shape[1]


def join_kernel(peers, *refs):
    whole = refs[-1]
    pad = refs[0].shape[0]
    me = lax.axis_index("dp")
    for step, ref in zip(far_first(peers), refs):
        whole[pl.ds(pl.multiple_of(step_to(step, me, peers) * pad, pad), pad), :] = ref[...]


def pair_kernel(peers, own_ref, returned_ref, after_ref, *outs):
    rows = own_ref.shape[0] // 2
    pad = rows // peers
    me = lax.axis_index("dp")
    for half in range(2):
        for step in range(peers):
            row = half * rows + step_to(step, me, peers) * pad
            at = pl.ds(pl.multiple_of(row, pad), pad)
            both = own_ref[at, :].astype(F32) + returned_ref[at, :].astype(F32)
            if half == 0:
                outs[0][step * pad : (step + 1) * pad, :] = both
            else:
                part, place = divmod(step * pad, outs[1].shape[0])
                outs[1 + part][place : place + pad, :] = both.astype(BF16)


def sum_kernel(parts, mine_ref, *refs):
    theirs, outs = refs[:parts], refs[parts + 1 :]
    pad = outs[0].shape[0]
    for step, out in enumerate(outs):
        part, place = divmod(step * pad, theirs[0].shape[0])
        out[...] = (
            mine_ref[step * pad : (step + 1) * pad, :]
            + theirs[part][place : place + pad, :].astype(F32)
        ).astype(BF16)


def call(kernel, outs, *args, scratch=(), in_specs=None, cost=None):
    return pl.pallas_call(
        kernel,
        out_shape=outs,
        in_specs=in_specs or [pl.BlockSpec(memory_space=pltpu.VMEM)] * len(args),
        scratch_shapes=scratch,
        compiler_params=pltpu.CompilerParams(vmem_limit_bytes=vmem_bytes),
        cost_estimate=cost,
    )(*args)


def local(queries, key_rows, value_rows, grad_out, doc_lengths, dest_index):
    row_count = queries.shape[1]
    peers = lax.axis_size("dp")
    span = lax.axis_size("seq")
    group_rows = row_count // peers
    pad = -(-group_rows // TILE) * TILE
    rows = peers * pad
    shape = jax.ShapeDtypeStruct

    sources = [
        pltpu.with_memory_space_constraint(a, pltpu.HBM)
        for a in (doc_lengths, dest_index, queries[0], key_rows[0], value_rows[0], grad_out[0])
    ]
    lengths, dest, q, k, v, g = sources
    *kv, slot, first_seen, q, g = call(
        functools.partial(sort_kernel, peers, pad),
        [shape((pad, 2 * HEAD_DIM), BF16)] * peers
        + [shape((1, row_count), jnp.int32), shape((1, 2 * rows), jnp.int32)]
        + [shape(q.shape, BF16)] * 2,
        lengths,
        dest,
        k,
        v,
        q,
        g,
        in_specs=[pl.BlockSpec(memory_space=pltpu.HBM)] * 6,
        scratch=[pltpu.SMEM(lengths.shape, jnp.int32), pltpu.VMEM(dest.shape, jnp.int32)]
        + [pltpu.VMEM((row_count, 2 * HEAD_DIM), BF16)]
        + [pltpu.SemaphoreType.DMA((6,))],
    )
    qg = call(
        functools.partial(follow_kernel, peers, pad),
        [shape((pad, 4 * HEAD_DIM), BF16)] * peers,
        slot,
        q,
        g,
        cost=pause,
    )

    def exchange(pieces, home=False, order=travel_order(peers)):
        arrived = []
        for k in order:
            way = [(i, receiver_of(i, k, peers)) for i in range(peers)]
            if home:
                way = [(j, i) for i, j in way]
            arrived.append(lax.ppermute(pieces[k], "dp", way) if k else pieces[k])
        return arrived

    def to_partner(values, distance):
        return lax.ppermute(values, "seq", [(i, i ^ distance) for i in range(span)])

    def join(pieces):
        return call(functools.partial(join_kernel, peers), shape((rows, 2 * HEAD_DIM), BF16), *pieces, cost=brief)

    kv = exchange(kv, order=far_first(peers))
    near_first = [1, *range(peers - 1, 1, -1), 0]
    qg = exchange(qg, order=near_first)
    sequence = lax.all_gather(join(kv), "seq", axis=0, tiled=True)
    back = call(back_kernel, shape((row_count, rows), BF16), slot)

    wide = (span * rows, 2 * rows)
    own_grad, far_grad, low, ds = call(
        functools.partial(attend_kernel, near_first, pad, row_count, span),
        [shape((2 * rows, 2 * HEAD_DIM), BF16)] * 2 + [shape(wide, BF16)] * 2,
        sequence,
        first_seen,
        *qg,
        scratch=[pltpu.VMEM(wide, F32)] * 2
        + [pltpu.VMEM((span * rows, HEAD_DIM), F32)] * 2
        + [pltpu.VMEM((2 * rows, HEAD_DIM), BF16)] * 2,
    )
    attended = call(
        functools.partial(gather_kernel, peers, pad, row_count, span),
        [shape((pad, 4 * HEAD_DIM), BF16)] * peers,
        sequence,
        low,
        ds,
        scratch=[pltpu.VMEM((2 * HEAD_DIM, 2 * rows), BF16), pltpu.VMEM((2 * rows, HEAD_DIM), BF16)],
    )

    returned = to_partner(far_grad, 1)
    parts = PARTS
    mine, *theirs = call(
        functools.partial(pair_kernel, peers),
        [shape((rows, 2 * HEAD_DIM), F32)] + [shape((rows // parts, 2 * HEAD_DIM), BF16)] * parts,
        own_grad,
        returned,
        attended[0],
        cost=pause,
    )
    attended = exchange(attended, home=True)
    pair_grad = call(
        functools.partial(sum_kernel, parts),
        [shape((pad, 2 * HEAD_DIM), BF16)] * peers,
        mine,
        *[to_partner(part, 2) for part in theirs],
        attended[0],
        cost=pause,
    )
    pair_grad = exchange(pair_grad, home=True)

    wide, narrow = shape((row_count, 2 * HEAD_DIM), BF16), shape((row_count, HEAD_DIM), BF16)
    first = call(
        functools.partial(settle_kernel, peers), [wide, wide], back, *attended
    )
    last = call(functools.partial(settle_kernel, peers), [narrow, narrow], back, *pair_grad)
    return first[0][None], first[1][None], last[0][None], last[1][None]


def solution(mesh):
    split = P("dp", "seq", "head")
    return jax.shard_map(
        local,
        mesh=mesh,
        in_specs=(split, split, split, split, P("dp", None), P("dp", "seq")),
        out_specs=(split, split, split, split),
        check_vma=False,
    )
```
